256 devices in a mesh: row: 2 (over core), blk: 128 (over y, z, x).
Axes of the slice: x: 4, y: 4, z: 8, core: 2. Of those that a mesh axis runs over, the one named last changes fastest.
Arguments:
- state: float32 [2, 5, 4096, 512], P('row', None, 'blk'), may hold values from -6 to 6
- forcing: float32 [2, 5, 4096, 512], P('row', None, 'blk'), may hold values from -6 to 6
- sigma: float32 [2, 4096, 512], P('row', 'blk'), may hold values from 0.05 to 2
- partner: int32 [2, 4096, 1], P('row', 'blk'), may hold values from 0 to 15; in each aligned block of 32 rows (0 to 31, 32 to 63, ..., all dimensions but the last counted through in order) at most 4 rows name the same one
- loop_weight: float32 [2, 1024], P('row'), may hold values from 0.05 to 0.2
- offset: int32 [1], replicated, may hold values from 0 to 1023
Outputs:
- solution: float32 [2, 5, 4096, 512], P('row', None, 'blk')
- loop_correction: float32 [2, 5, 1024], P('row', None, 'blk')
The draws below stay inside these ranges and needn't reach their ends.
Inputs may be any that keep to these rules, and one draw needn't show every extreme that they name: Among the 32 face cells of one device no partner slot is named more than 4 times.
All inputs are finite; a program needn't handle non-finite values.
Results may differ from the reference program's by a relative error of at most 0.00011.
Values sent between devices are 32-bit elements; how exact they have to be, the bound alone decides.
A program may use at most 64 MiB of HBM per device.

```python
import math
import jax
import jax.numpy as jnp
import numpy as np

V = 5
CI = 32
CJ = 512
SECTIONS1 = 3
SECTIONS2 = 3
SECTIONS3 = 4
MOST = 4
LOOP_SLOTS = 16
NI = 4096
NRING = 1024


def shard_levels(rng, dims, cuts, least, largest):
    loudness, own = 1.0, jax.random.fold_in(rng, 6)
    for position, blocks in cuts:
        draws = jnp.exp(jax.random.uniform(jax.random.fold_in(own, position), (blocks,), jnp.float32, least / len(cuts), largest / len(cuts)))
        loudness = loudness * jnp.repeat(draws, dims[position] // blocks).reshape([-1 if axis == position else 1 for axis in range(len(dims))])
    return loudness


def shared_out(stream_key, own, number, rows, amount, top, reach, slope):
    ranking = jax.random.permutation(stream_key, amount)
    heavy_load, common = load_shares(amount, rows * top, reach, slope, True), load_shares(amount, rows * top, reach, slope, False)
    places = jnp.arange(amount)

    def named(lengths, offset_by):
        used = int((lengths > 0).sum())
        fixed = max(1, used // 4)
        passed = fixed + (places - fixed + offset_by * (used - fixed)) % max(1, amount - fixed)
        return jnp.zeros((amount,), jnp.int32).at[ranking[jnp.where(places < fixed, places, passed)]].set(jnp.asarray(lengths, jnp.int32))

    lengths = jnp.where(number % 4 == 0, named(heavy_load, number // 4), named(common, number - number // 4 - 1))
    mixed = jax.random.permutation(jax.random.fold_in(own, 3), amount)
    donor, taker = mixed[0:amount // 2 * 2:2], mixed[1:amount // 2 * 2:2]
    margin = jnp.minimum(lengths[donor] - 1, reach - lengths[taker]) // 2
    margin = jnp.where((donor == ranking[0]) | (taker == ranking[0]) | (lengths[taker] == 0), 0, jnp.maximum(margin, 0))
    passed = jax.random.randint(jax.random.fold_in(own, 4), (amount // 2,), 0, 1 << 20) % (margin + 1)
    lengths = lengths.at[donor].add(-passed).at[taker].add(passed)
    members = jnp.searchsorted(jnp.cumsum(lengths), jnp.arange(rows * top), side="right").astype(jnp.int32)
    grid = members.reshape(top, rows).T
    grid = grid[jax.random.permutation(jax.random.fold_in(own, 1), rows)]
    offset_by = jax.random.randint(jax.random.fold_in(own, 2), (rows, 1), 0, top)
    return jnp.take_along_axis(grid, (jnp.arange(top)[None, :] + offset_by) % top, axis=1)


def load_shares(count, total, bound, slope, full):
    portions = [(1 << 20) // math.isqrt(grade ** slope) + 1 for grade in range(1, count + 1)]
    largest = bound if full else min(bound, max(-(-total // count), total * portions[0] // sum(portions)))
    least = 1 if total - largest >= count - 1 else 0
    counts, rest = [largest] + [least] * (count - 1), total - largest - least * (count - 1)
    while rest > 0:
        candidates = [i for i in range(1, count) if counts[i] < largest] or [i for i in range(1, count) if counts[i] < bound]
        mass, left = sum([portions[i] for i in candidates]), rest
        for i in candidates:
            more = min(bound - counts[i], max(1, left * portions[i] // mass), rest)
            counts[i] = counts[i] + more
            rest = rest - more
    return np.array(counts)


def scatter_about(own_key, dims, deviation, limit, split=(), held_as=jnp.bfloat16):
    entries = deviation * jax.random.normal(own_key, dims, jnp.float32)
    if split:
        entries = entries * shard_levels(own_key, dims, split, -0.22, 0.18)
    return jnp.clip(entries, -limit, limit).astype(held_as)


def setup_inputs(seed: int = 0) -> dict:
    seeds = jax.random.split(jax.random.key(seed), 7)
    state = scatter_about(seeds[0], (2, V, NI, CJ), 1.0, 6.0, ((0, 2), (2, 128)), jnp.float32)
    forcing = scatter_about(seeds[1], (2, V, NI, CJ), 1.0, 6.0, ((0, 2), (2, 128)), jnp.float32)
    sigma = jnp.clip(jnp.exp(math.log(2.0) - 3.6888794 * jax.random.uniform(seeds[2], (2, NI, CJ), jnp.float32) ** shard_levels(seeds[2], (2, NI, CJ), ((0, 2), (1, 128)), -0.2, 0.2)), 0.05, 2.0)
    partner_keys = jax.random.split(jax.random.fold_in(seeds[3], 1), 2 * NI // CI)
    partner_turns = jax.random.permutation(jax.random.fold_in(seeds[3], 3), 2 * NI // CI)
    partner = jax.vmap(lambda own, number: shared_out(jax.random.fold_in(seeds[3], 2), own, number, CI, LOOP_SLOTS, 1, MOST, 2))(partner_keys, partner_turns).reshape((2, NI, 1))
    loop_weight = jnp.clip(jnp.exp(math.log(0.2) - 1.3862944 * jax.random.uniform(seeds[4], (2, NRING), jnp.float32) ** shard_levels(seeds[4], (2, NRING), ((0, 2),), -0.2, 0.2)), 0.05, 0.2)
    offset = jax.random.randint(seeds[5], (1,), 0, NRING).astype(jnp.int32)
    return dict(state=state, forcing=forcing, sigma=sigma, partner=partner, loop_weight=loop_weight, offset=offset)


COEFF = 0.8


def nonlinear(field):
    q = jnp.mean(field * field, axis=0, keepdims=True)
    return 0.5 * field * q / (1.0 + q)


def operator(field, sigma_in, scale):
    across = jnp.roll(field, 1, axis=1) + jnp.roll(field, -1, axis=1)
    padded = jnp.pad(field, ((0, 0), (0, 0), (1, 1)))
    along = padded[:, :, 2:] + padded[:, :, :-2]
    return scale * (4.0 * field - (across + along)) + sigma_in[None] * field + nonlinear(field)


def smooth(field, source, sigma_in, scale, count):
    tau = (COEFF / (4.0 * scale + sigma_in + 1.5))[None]
    start = field
    for section in range(count):
        field = start + (1.0 / (count - section)) * tau * (source - operator(field, sigma_in, scale))
    return field


def coarsen(x):
    rows, cols = x.shape[-2], x.shape[-1]
    return x.reshape(x.shape[:-2] + (rows // 2, 2, cols // 2, 2)).mean(axis=(-3, -1))


def refine(x):
    return jnp.repeat(jnp.repeat(x, 2, axis=-2), 2, axis=-1)


def loop_cells_of(partner_row):
    blocks = NI // CI
    owner_block = (jnp.arange(NI, dtype=jnp.int32) // CI).astype(jnp.int32)
    return ((partner_row * blocks + owner_block) % NRING).astype(jnp.int32)


def reference(state, forcing, sigma, partner, loop_weight, offset):
    fine_states = []
    fine_resid = []
    sums = []
    cells = []
    for row in range(2):
        u1 = smooth(state[row], forcing[row], sigma[row], 1.0, SECTIONS1)
        r1 = forcing[row] - operator(u1, sigma[row], 1.0)
        if row == 0:
            face = r1[:, :, -1]
        else:
            face = r1[:, :, 0]
        loop_cell = loop_cells_of(partner[row, :, 0])
        cells.append(loop_cell)
        sums.append(jax.ops.segment_sum(face.T, loop_cell, num_segments=NRING).T)
        fine_states.append(u1)
        fine_resid.append(r1)
    shift = offset[0]
    corr_rotor = loop_weight[0][None, :] * (sums[0] + jnp.roll(sums[1], -shift, axis=1))
    corr_stator = loop_weight[1][None, :] * (sums[1] + jnp.roll(sums[0], shift, axis=1))
    corrections = [corr_rotor, corr_stator]
    results = []
    for row in range(2):
        u1 = fine_states[row]
        r1 = fine_resid[row]
        s1 = sigma[row]
        s2 = coarsen(s1)
        s3 = coarsen(s2)
        u2_start = coarsen(u1)
        f2 = operator(u2_start, s2, 0.25) + coarsen(r1)
        u2 = smooth(u2_start, f2, s2, 0.25, SECTIONS2)
        r2 = f2 - operator(u2, s2, 0.25)
        u3_start = coarsen(u2)
        f3 = operator(u3_start, s3, 0.0625) + coarsen(r2)
        u3 = smooth(u3_start, f3, s3, 0.0625, SECTIONS3)
        u2 = u2 + refine(u3 - u3_start)
        u2 = smooth(u2, f2, s2, 0.25, SECTIONS2)
        u1 = u1 + refine(u2 - u2_start)
        fix = corrections[row][:, cells[row]]
        column = CJ - 1 if row == 0 else 0
        u1 = u1.at[:, :, column].add(fix)
        u1 = smooth(u1, forcing[row], s1, 1.0, SECTIONS1)
        results.append(u1)
    return jnp.stack(results), jnp.stack(corrections)
```

```python
import jax
import jax.numpy as jnp
from jax import lax
from jax.experimental import pallas as pl
from jax.experimental.pallas import tpu as pltpu
from jax.sharding import PartitionSpec as P

MESH = pl.DeviceIdType.MESH
V = 5
NB = 128
O1, R1 = 16, 64
O2, R2 = 24, 64
O3, R3 = 16, 40
NY, NZ, NX = 4, 8, 4
HIGH = lax.Precision.HIGHEST


def loop(first, tiles, body):
    def step(k, carry):
        body(first + 8 * k)
        return carry

    lax.fori_loop(0, tiles, step, 0)


def lanes(shape=(8, 128)):
    return lax.broadcasted_iota(jnp.int32, shape, 1)


def rows_of(shape=(8, 128)):
    return lax.broadcasted_iota(jnp.int32, shape, 0)


def apply_l(u_ref, s_ref, r, nt, scale):
    lane = lanes()
    first, last = lane == 0, lane == 127
    here = pl.ds(r, 8)
    centre = [[u_ref[v, t, here, :] for t in range(nt)] for v in range(V)]
    out = [[None] * nt for _ in range(V)]
    diag = []
    for t in range(nt):
        q = centre[0][t] * centre[0][t]
        for v in range(1, V):
            q = q + centre[v][t] * centre[v][t]
        q = q * (1.0 / V)
        diag.append((s_ref[t, here, :] + 4.0 * scale) + (0.5 * q) / (1.0 + q))
    for v in range(V):
        ahead = [pltpu.roll(centre[v][t], 127, 1) for t in range(nt)]
        behind = [pltpu.roll(centre[v][t], 1, 1) for t in range(nt)]
        for t in range(nt):
            right = jnp.where(last, ahead[t + 1] if t + 1 < nt else 0.0, ahead[t])
            left = jnp.where(first, behind[t - 1] if t > 0 else 0.0, behind[t])
            near = (right + left) + (
                u_ref[v, t, pl.ds(r - 1, 8), :] + u_ref[v, t, pl.ds(r + 1, 8), :]
            )
            if scale != 1.0:
                near = scale * near
            out[v][t] = diag[t] * centre[v][t] - near
    return centre, out


def section(dst, start, src, f_ref, s_ref, tau_ref, first, tiles, nt, scale, portion, shift=0):
    def body(r):
        here = pl.ds(r, 8)
        _, out = apply_l(src, s_ref, r, nt, scale)
        for t in range(nt):
            tau = tau_ref[t, here, :] * portion
            for v in range(V):
                dst[v, t, pl.ds(r - shift, 8), :] = start[v, t, here, :] + tau * (
                    f_ref[v, t, here, :] - out[v][t]
                )

    loop(first, tiles, body)


def step_size(tau_ref, s_ref, first, tiles, nt, scale):
    def body(r):
        for t in range(nt):
            tau_ref[t, pl.ds(r, 8), :] = 0.8 / (s_ref[t, pl.ds(r, 8), :] + (4.0 * scale + 1.5))

    loop(first, tiles, body)


def halved(a, b, pick):
    lane = lanes()
    mixed = jnp.where(lane % 2 == 0, a + pltpu.roll(a, 127, 1), b + pltpu.roll(b, 1, 1))
    return jnp.take_along_axis(mixed, pick, axis=1)


def pair_pick():
    lane = lanes()
    return jnp.where(lane < 64, 2 * lane, 2 * lane - 127)


def coarsen_rows(get, f, nt, pick):
    pairs = [get(t, pl.ds(f, 8, stride=2)) + get(t, pl.ds(f + 1, 8, stride=2)) for t in range(nt)]
    if nt == 1:
        return [halved(pairs[0], jnp.zeros_like(pairs[0]), pick) * 0.25]
    return [halved(pairs[2 * t], pairs[2 * t + 1], pick) * 0.25 for t in range(nt // 2)]


def kernel(
    state, forcing, sigma, partner, weight, offset, out, loop_out,
    u1a, u1b, u1c, u1d, f1, s1, t1, outb,
    u2a, u2b, u2c, u2d, r2c, f2, s2, t2,
    u3a, u3b, u3c, r3c, f3, s3, t3,
    onehot, wrow, swap, swapped, comb, zrows, table,
    load_sem, a_send, a_recv, b_send, b_recv, g_send, g_recv, out_sem,
):
    row = lax.axis_index("row")
    b = lax.axis_index("blk")
    right, left = lax.rem(b + 1, NB), lax.rem(b + NB - 1, NB)
    y, z, x = b // 32, lax.rem(b // 4, NZ), lax.rem(b, NX)
    me = y * NX + x
    beside = [(row, right), (row, left)]
    z_peers = [(row, y * 32 + lax.rem(z + d, NZ) * 4 + x) for d in range(1, NZ)]
    xy_peers = [
        (row, lax.rem(y + dy, NY) * 32 + z * 4 + lax.rem(x + dx, NX))
        for dy in range(NY)
        for dx in range(NX)
        if dx or dy
    ]
    partners = beside + [(1 - row, b)] + z_peers + xy_peers
    barrier = pltpu.get_barrier_semaphore()
    for device in partners:
        pl.semaphore_signal(barrier, inc=1, device_id=device, device_id_type=MESH)

    loads = []
    for t in range(4):
        cols = pl.ds(t * 128, 128)
        own = pl.ds(O1, 32)
        loads.append((sigma.at[0, :, cols], s1.at[t, own, :]))
        loads.append((state.at[0, :, :, cols], u1a.at[:, t, own, :]))
        loads.append((forcing.at[0, :, :, cols], f1.at[:, t, own, :]))
    loads = [pltpu.make_async_copy(src, dst, load_sem.at[i]) for i, (src, dst) in enumerate(loads)]
    for copy in loads:
        copy.start()

    lane = lanes()
    pick = pair_pick()
    low = lane % 8
    for k in range(4):
        slot = lax.rem(partner[0, pl.ds(8 * k, 8), :], 8)
        onehot[pl.ds(O1 + 8 * k, 8), :] = (slot == low).astype(jnp.float32)
    weights = jnp.zeros((8, 128), jnp.float32)
    for d, block in enumerate((left, b, right)):
        for p in range(8):
            weights = jnp.where((rows_of() == d) & (low == p), weight[0, p * NB + block], weights)
    wrow[...] = weights

    for copy in loads:
        copy.wait()
    for k in range(2):
        r = O2 + 8 * k
        for t, tile in enumerate(coarsen_rows(lambda t, rows: s1[t, rows, :], O1 + 16 * k, 4, pick)):
            s2[t, pl.ds(r, 8), :] = tile
    pl.semaphore_wait(barrier, len(partners))

    def across(ref, lead, sources, targets, send, recv, first):
        copies = []
        for d in range(2):
            src = ref.at[(slice(None),) * lead + (pl.ds(*sources[d]), slice(None))]
            dst = ref.at[(slice(None),) * lead + (pl.ds(*targets[d]), slice(None))]
            copies.append(
                pltpu.make_async_remote_copy(
                    src_ref=src, dst_ref=dst, send_sem=send.at[first + d], recv_sem=recv.at[first + d],
                    device_id=beside[d], device_id_type=MESH,
                )
            )
        for copy in copies:
            copy.start()
        return copies

    def fine(ref, lead, n, first):
        return across(
            ref, lead, ((O1 + 32 - n, n), (O1, n)), ((O1 - n, n), (O1 + 32, n)), a_send, a_recv, first
        )

    wide = ((O2, 16), (O2, 16)), ((O2 - 16, 16), (O2 + 16, 16))
    a_copies = fine(u1a, 2, 6, 0) + fine(f1, 2, 5, 2) + fine(s1, 1, 5, 4)
    a_late = fine(onehot, 0, 4, 6)
    b_early = across(s2, 1, *wide, b_send, b_recv, 0)
    for copy in a_copies:
        copy.wait_recv()

    step_size(t1, s1, O1 - 8, 6, 4, 1.0)
    section(u1b, u1a, u1a, f1, s1, t1, O1 - 8, 6, 4, 1.0, 1.0 / 3.0)
    section(u1c, u1a, u1b, f1, s1, t1, O1 - 4, 5, 4, 1.0, 0.5)
    section(u1b, u1a, u1c, f1, s1, t1, O1 - 4, 5, 4, 1.0, 1.0)

    target = jnp.where(row == 0, 127, 0)
    at_target = jnp.zeros((8, 128), jnp.int32) + target
    variable = (lane - 64 * row) // 8
    inside = lane >= 64 * row
    swap[...] = jnp.zeros((8, 128), jnp.float32)

    def residual(r):
        here = pl.ds(r, 8)
        _, out_l = apply_l(u1b, s1, r, 4, 1.0)
        mixed = jnp.zeros((8, 128), jnp.float32)
        for v in range(V):
            rest = [f1[v, t, here, :] - out_l[v][t] for t in range(4)]
            for t in range(4):
                u1c[v, t, here, :] = rest[t]
            face = jnp.take_along_axis(jnp.where(row == 0, rest[3], rest[0]), at_target, axis=1)
            mixed = jnp.where((variable == v) & inside, face, mixed)
        swap[...] += mixed * onehot[here, :]

    loop(O1, 4, residual)
    total = jnp.sum(swap[...], axis=0, keepdims=True)
    comb[0:1, :] = total
    to_core = pltpu.make_async_remote_copy(
        src_ref=comb.at[0:1, :], dst_ref=swapped.at[0:1, :], send_sem=g_send.at[0], recv_sem=g_recv.at[0],
        device_id=(1 - row, b), device_id_type=MESH,
    )
    to_core.start()

    for k, r in enumerate((-1, 7, 9)):
        for v in range(V):
            tiles = coarsen_rows(lambda t, rows, v=v: u1b[v, t, rows, :], O1 + 2 * r, 4, pick)
            for t in range(2):
                u2a[v, t, pl.ds(O2 + r, 8), :] = tiles[t]
    for r in (0, 8):
        for v in range(V):
            tiles = coarsen_rows(lambda t, rows, v=v: u1c[v, t, rows, :], O1 + 2 * r, 4, pick)
            for t in range(2):
                r2c[v, t, pl.ds(O2 + r, 8), :] = tiles[t]
    b_copies = across(
        u2a, 2, ((O2 - 1, 16), (O2 + 1, 16)), ((O2 - 17, 16), (O2 + 17, 16)), b_send, b_recv, 2
    )
    b_copies += across(r2c, 2, *wide, b_send, b_recv, 4)

    to_core.wait_recv()
    both = comb[0:1, :] + swapped[0:1, :]
    comb[1:2, :] = both
    zrows[pl.ds(z, 1), :] = both
    z_copies = [
        pltpu.make_async_remote_copy(
            src_ref=comb.at[1:2, :], dst_ref=zrows.at[pl.ds(z, 1), :], send_sem=g_send.at[1],
            recv_sem=g_recv.at[1], device_id=device, device_id_type=MESH,
        )
        for device in z_peers
    ]
    for copy in z_copies:
        copy.start()
    z_all = pltpu.make_async_remote_copy(
        src_ref=zrows.at[0 : NZ - 1, :], dst_ref=zrows.at[0 : NZ - 1, :], send_sem=g_send.at[1],
        recv_sem=g_recv.at[1], device_id=z_peers[0], device_id_type=MESH,
    )
    z_all.wait_recv()
    table[me] = zrows[...]
    t_copies = [
        pltpu.make_async_remote_copy(
            src_ref=zrows, dst_ref=table.at[me], send_sem=g_send.at[2],
            recv_sem=g_recv.at[2], device_id=device, device_id_type=MESH,
        )
        for device in xy_peers
    ]
    for copy in t_copies:
        copy.start()
    t_all = pltpu.make_async_remote_copy(
        src_ref=table.at[0 : NX * NY - 1], dst_ref=table.at[0 : NX * NY - 1], send_sem=g_send.at[2],
        recv_sem=g_recv.at[2], device_id=xy_peers[0], device_id_type=MESH,
    )

    for copy in b_early + b_copies:
        copy.wait_recv()
    step_size(t2, s2, O2 - 16, 6, 2, 0.25)
    portion = 1.0 / 3.0

    def middle_first(r):
        here = pl.ds(r, 8)
        centre, out_l = apply_l(u2a, s2, r, 2, 0.25)
        for t in range(2):
            tau = t2[t, here, :] * portion
            for v in range(V):
                rest = r2c[v, t, here, :]
                f2[v, t, here, :] = out_l[v][t] + rest
                u2b[v, t, here, :] = centre[v][t] + tau * rest

    loop(O2 - 16, 6, middle_first)
    section(u2c, u2a, u2b, f2, s2, t2, O2 - 16, 6, 2, 0.25, 0.5)
    section(u2b, u2a, u2c, f2, s2, t2, O2 - 16, 6, 2, 0.25, 1.0)

    def middle_rest(r):
        here = pl.ds(r, 8)
        _, out_l = apply_l(u2b, s2, r, 2, 0.25)
        for t in range(2):
            for v in range(V):
                u2c[v, t, here, :] = f2[v, t, here, :] - out_l[v][t]

    loop(O2 - 12, 5, middle_rest)

    for k in range(3):
        r, f = O3 - 8 + 8 * k, O2 - 16 + 16 * k
        here = pl.ds(r, 8)
        s3[0, here, :] = coarsen_rows(lambda t, rows: s2[t, rows, :], f, 2, pick)[0]
        t3[0, here, :] = 0.8 / (s3[0, here, :] + 1.75)
        for v in range(V):
            u3a[v, 0, here, :] = coarsen_rows(lambda t, rows, v=v: u2b[v, t, rows, :], f, 2, pick)[0]
            r3c[v, 0, here, :] = coarsen_rows(lambda t, rows, v=v: u2c[v, t, rows, :], f, 2, pick)[0]

    def coarse_first(r):
        here = pl.ds(r, 8)
        centre, out_l = apply_l(u3a, s3, r, 1, 0.0625)
        tau = t3[0, here, :] * 0.25
        for v in range(V):
            rest = r3c[v, 0, here, :]
            f3[v, 0, here, :] = out_l[v][0] + rest
            u3b[v, 0, here, :] = centre[v][0] + tau * rest

    loop(O3 - 8, 3, coarse_first)
    section(u3c, u3a, u3b, f3, s3, t3, O3 - 8, 3, 1, 0.0625, 1.0 / 3.0)
    section(u3b, u3a, u3c, f3, s3, t3, O3 - 4, 2, 1, 0.0625, 0.5)
    section(u3c, u3a, u3b, f3, s3, t3, O3 - 4, 2, 1, 0.0625, 1.0)

    spread = [lane // 2, 64 + lane // 2]
    for k in range(2):
        r, f = O3 - 4 + 8 * k, O2 - 8 + 16 * k
        for v in range(V):
            gain = u3c[v, 0, pl.ds(r, 8), :] - u3a[v, 0, pl.ds(r, 8), :]
            for t in range(2):
                more = jnp.take_along_axis(gain, spread[t], axis=1)
                for odd in range(2):
                    rows = pl.ds(f + odd, 8, stride=2)
                    u2d[v, t, rows, :] = u2b[v, t, rows, :] + more

    section(u2b, u2d, u2d, f2, s2, t2, O2 - 4, 3, 2, 0.25, 1.0 / 3.0)
    section(u2c, u2d, u2b, f2, s2, t2, O2 - 4, 3, 2, 0.25, 0.5)
    section(u2b, u2d, u2c, f2, s2, t2, O2 - 4, 3, 2, 0.25, 1.0)

    for r in (-2, 6, 10):
        f = O1 + 2 * r
        for v in range(V):
            for half in range(2):
                here = pl.ds(O2 + r, 8)
                gain = u2b[v, half, here, :] - u2a[v, half, here, :]
                for part in range(2):
                    t = 2 * half + part
                    more = jnp.take_along_axis(gain, spread[part], axis=1)
                    for odd in range(2):
                        rows = pl.ds(f + odd, 8, stride=2)
                        u1d[v, t, rows, :] = u1b[v, t, rows, :] + more

    for copy in a_late:
        copy.wait_recv()
    t_all.wait_recv()

    turn = jnp.where(row == 0, offset[0], 1024 - offset[0])
    index = rows_of()
    cell_own = 8 * b + index
    near_own = lax.rem(b + NB - 1 + index, NB)
    cell_other = (cell_own + turn) & 1023
    near_other = (near_own + turn) & 1023

    def chosen(block):
        block = block & 127
        place = ((block >> 5) * 4 + (block & 3)) * 8 + ((block >> 2) & 7)
        return (place == lane).astype(jnp.float32)

    wanted = jnp.concatenate(
        [chosen(cell_own), chosen(near_own), chosen(cell_other), chosen(near_other)], axis=0
    )
    found = jnp.dot(
        wanted, table[...].reshape(NB, 128), precision=HIGH, preferred_element_type=jnp.float32
    )
    turned = pltpu.roll(found, 64, 1)
    own = jnp.where(row == 0, found[0:16], turned[0:16])
    other = jnp.where(row == 0, turned[16:32], found[16:32])
    valid = lane < 40
    picked = jnp.where(valid & (low == (b // 16)), own[0:8], 0.0) + jnp.where(
        valid & (low == (cell_other >> 7)), other[0:8], 0.0
    )
    summed = (index == lane // 8).astype(jnp.float32)
    cells = lax.dot_general(
        summed, picked, (((1,), (1,)), ((), ())), precision=HIGH, preferred_element_type=jnp.float32
    )
    scale8 = jnp.zeros((8, 8), jnp.float32)
    for k in range(8):
        scale8 = jnp.where(lanes((8, 8)) == k, weight[0, 8 * b + k], scale8)
    loop_out[0] = (cells * scale8)[0:V]

    rotate = (lane & ~7) | ((lane + (near_other >> 7)) & 7)
    corr = jnp.where(
        valid, wrow[...] * (own[8:16] + jnp.take_along_axis(other[8:16], rotate, axis=1)), 0.0
    )
    swap[...] = corr
    first_col = (lane == 0) & (row == 1)
    last_col = (lane == 127) & (row == 0)
    for k in range(5):
        r = O1 - 4 + 8 * k
        here = pl.ds(r, 8)
        near = index + r
        if k == 0:
            table_row = jnp.where(near < O1, swap[0:1, :], swap[1:2, :])
        elif k == 4:
            table_row = jnp.where(near < O1 + 32, swap[1:2, :], swap[2:3, :])
        else:
            table_row = swap[1:2, :]
        terms = onehot[here, :] * table_row
        for hop in (4, 2, 1):
            terms = terms + pltpu.roll(terms, 128 - hop, 1)
        for v in range(V):
            fix = jnp.take_along_axis(terms, jnp.full((8, 128), 8 * v, jnp.int32), axis=1)
            u1d[v, 0, here, :] += jnp.where(first_col, fix, 0.0)
            u1d[v, 3, here, :] += jnp.where(last_col, fix, 0.0)

    section(u1c, u1d, u1d, f1, s1, t1, O1 - 4, 5, 4, 1.0, 1.0 / 3.0)
    section(u1b, u1d, u1c, f1, s1, t1, O1 - 4, 5, 4, 1.0, 0.5)
    section(outb, u1d, u1b, f1, s1, t1, O1, 4, 4, 1.0, 1.0, shift=O1)

    stores = [
        pltpu.make_async_copy(outb.at[:, t], out.at[0, :, :, pl.ds(t * 128, 128)], out_sem.at[t])
        for t in range(4)
    ]
    for copy in stores:
        copy.start()
    for copy in a_copies + a_late + b_early + b_copies + [to_core]:
        copy.wait_send()
    z_all.wait_send()
    t_all.wait_send()
    for copy in stores:
        copy.wait()


def body(state, forcing, sigma, partner, loop_weight, offset):
    f32 = jnp.float32
    fine, middle, coarse = (V, 4, R1, 128), (V, 2, R2, 128), (V, 1, R3, 128)
    buffers = [fine] * 5 + [(4, R1, 128)] * 2 + [(V, 4, 32, 128)]
    buffers += [middle] * 6 + [(2, R2, 128)] * 2
    buffers += [coarse] * 5 + [(1, R3, 128)] * 2
    buffers += [(R1, 128), (8, 128), (8, 128), (8, 128), (8, 128), (NZ, 128), (NX * NY, NZ, 128)]
    any_space = pl.BlockSpec(memory_space=pl.ANY)
    smem = pl.BlockSpec(memory_space=pltpu.SMEM)
    vmem = pl.BlockSpec(memory_space=pltpu.VMEM)
    dma = pltpu.SemaphoreType.DMA
    return pl.pallas_call(
        kernel,
        out_shape=(
            jax.ShapeDtypeStruct((1, V, 32, 512), f32),
            jax.ShapeDtypeStruct((1, V, 8), f32),
        ),
        in_specs=[any_space, any_space, any_space, vmem, smem, smem],
        out_specs=(any_space, vmem),
        scratch_shapes=[pltpu.VMEM(shape, f32) for shape in buffers]
        + [dma((12,)), dma((8,)), dma((8,)), dma((6,)), dma((6,)), dma((3,)), dma((3,)), dma((4,))],
        compiler_params=pltpu.CompilerParams(
            collective_id=0, has_side_effects=True, vmem_limit_bytes=40 * 1024 * 1024
        ),
        name="fas_cycle",
    )(state, forcing, sigma, partner, loop_weight, offset)


def solution(mesh):
    placed = (
        P("row", None, "blk", None),
        P("row", None, "blk", None),
        P("row", "blk", None),
        P("row", "blk", None),
        P("row", None),
        P(),
    )
    return jax.shard_map(
        body,
        mesh=mesh,
        in_specs=placed,
        out_specs=(P("row", None, "blk", None), P("row", None, "blk")),
        check_vma=False,
    )
```

```python
import jax
import jax.numpy as jnp
from jax import lax
from jax.experimental import pallas as pl
from jax.experimental.pallas import tpu as pltpu
from jax.sharding import PartitionSpec as P

MESH = pl.DeviceIdType.MESH
V = 5
NB = 128
O1, R1 = 16, 64
O2, R2 = 24, 64
O3, R3 = 16, 40
NY, NZ, NX = 4, 8, 4
HIGH = lax.Precision.HIGHEST


def loop(first, tiles, body):
    def step(k, carry):
        body(first + 8 * k)
        return carry

    lax.fori_loop(0, tiles, step, 0, unroll=2 if tiles % 2 == 0 else 1)


def lanes(shape=(8, 128)):
    return lax.broadcasted_iota(jnp.int32, shape, 1)


def rows_of(shape=(8, 128)):
    return lax.broadcasted_iota(jnp.int32, shape, 0)


def apply_l(u_ref, s_ref, r, nt, scale):
    lane = lanes()
    first, last = lane == 0, lane == 127
    here = pl.ds(r, 8)
    centre = [[u_ref[v, t, here, :] for t in range(nt)] for v in range(V)]
    out = [[None] * nt for _ in range(V)]
    diag = []
    for t in range(nt):
        q = centre[0][t] * centre[0][t]
        for v in range(1, V):
            q = q + centre[v][t] * centre[v][t]
        q = q * (1.0 / V)
        diag.append((s_ref[t, here, :] + 4.0 * scale) + (0.5 * q) / (1.0 + q))
    for v in range(V):
        ahead = [pltpu.roll(centre[v][t], 127, 1) for t in range(nt)]
        behind = [pltpu.roll(centre[v][t], 1, 1) for t in range(nt)]
        for t in range(nt):
            right = jnp.where(last, ahead[t + 1] if t + 1 < nt else 0.0, ahead[t])
            left = jnp.where(first, behind[t - 1] if t > 0 else 0.0, behind[t])
            near = (right + left) + (
                u_ref[v, t, pl.ds(r - 1, 8), :] + u_ref[v, t, pl.ds(r + 1, 8), :]
            )
            if scale != 1.0:
                near = scale * near
            out[v][t] = diag[t] * centre[v][t] - near
    return centre, out


def section(dst, start, src, f_ref, s_ref, tau_ref, first, tiles, nt, scale, portion, shift=0):
    def body(r):
        here = pl.ds(r, 8)
        _, out = apply_l(src, s_ref, r, nt, scale)
        for t in range(nt):
            tau = tau_ref[t, here, :] * portion
            for v in range(V):
                dst[v, t, pl.ds(r - shift, 8), :] = start[v, t, here, :] + tau * (
                    f_ref[v, t, here, :] - out[v][t]
                )

    loop(first, tiles, body)


def step_size(tau_ref, s_ref, first, tiles, nt, scale):
    def body(r):
        for t in range(nt):
            tau_ref[t, pl.ds(r, 8), :] = 0.8 / (s_ref[t, pl.ds(r, 8), :] + (4.0 * scale + 1.5))

    loop(first, tiles, body)


def halved(a, b, pick):
    lane = lanes()
    mixed = jnp.where(lane % 2 == 0, a + pltpu.roll(a, 127, 1), b + pltpu.roll(b, 1, 1))
    return jnp.take_along_axis(mixed, pick, axis=1)


def pair_pick():
    lane = lanes()
    return jnp.where(lane < 64, 2 * lane, 2 * lane - 127)


def coarsen_rows(get, f, nt, pick):
    pairs = [get(t, pl.ds(f, 8, stride=2)) + get(t, pl.ds(f + 1, 8, stride=2)) for t in range(nt)]
    if nt == 1:
        return [halved(pairs[0], jnp.zeros_like(pairs[0]), pick) * 0.25]
    return [halved(pairs[2 * t], pairs[2 * t + 1], pick) * 0.25 for t in range(nt // 2)]


def kernel(
    state, forcing, sigma, partner_in, weight_in, offset, out, loop_out,
    u1a, u1b, u1c, u1d, f1, s1, t1, outb,
    u2a, u2b, u2c, u2d, r2c, f2, s2, t2,
    u3a, u3b, u3c, r3c, f3, s3, t3,
    onehot, wrow, swap, swapped, comb, zrows, table, partner, weight,
    load_sem, a_send, a_recv, b_send, b_recv, g_send, g_recv, out_sem,
):
    row = lax.axis_index("row")
    b = lax.axis_index("blk")
    right, left = lax.rem(b + 1, NB), lax.rem(b + NB - 1, NB)
    y, z, x = b // 32, lax.rem(b // 4, NZ), lax.rem(b, NX)
    me = y * NX + x
    beside = [(row, right), (row, left)]
    z_peers = [(row, y * 32 + lax.rem(z + d, NZ) * 4 + x) for d in range(1, NZ)]
    xy_peers = [
        (row, lax.rem(y + dy, NY) * 32 + z * 4 + lax.rem(x + dx, NX))
        for dy in range(NY)
        for dx in range(NX)
        if dx or dy
    ]
    partners = beside + [(1 - row, b)] + z_peers + xy_peers
    barrier = pltpu.get_barrier_semaphore()
    for device in partners:
        pl.semaphore_signal(barrier, inc=1, device_id=device, device_id_type=MESH)

    loads = []
    for t in range(4):
        cols = pl.ds(t * 128, 128)
        own = pl.ds(O1, 32)
        loads.append((sigma.at[0, :, cols], s1.at[t, own, :]))
        loads.append((state.at[0, :, :, cols], u1a.at[:, t, own, :]))
        loads.append((forcing.at[0, :, :, cols], f1.at[:, t, own, :]))
    loads = [(partner_in, partner), (weight_in, weight)] + loads
    loads = [pltpu.make_async_copy(src, dst, load_sem.at[i]) for i, (src, dst) in enumerate(loads)]
    for copy in loads:
        copy.start()
    for copy in loads[:2]:
        copy.wait()

    lane = lanes()
    pick = pair_pick()
    low = lane % 8
    for k in range(4):
        slot = jnp.zeros((8, 128), jnp.int32)
        for i in range(8):
            slot = jnp.where(rows_of() == i, partner[0, 0, 8 * k + i] & 7, slot)
        onehot[pl.ds(O1 + 8 * k, 8), :] = (slot == low).astype(jnp.float32)
    weights = jnp.zeros((8, 128), jnp.float32)
    for d, block in enumerate((left, b, right)):
        for p in range(8):
            weights = jnp.where((rows_of() == d) & (low == p), weight[0, p * NB + block], weights)
    wrow[...] = weights

    for copy in loads[2:]:
        copy.wait()
    for k in range(2):
        r = O2 + 8 * k
        for t, tile in enumerate(coarsen_rows(lambda t, rows: s1[t, rows, :], O1 + 16 * k, 4, pick)):
            s2[t, pl.ds(r, 8), :] = tile
    pl.semaphore_wait(barrier, len(partners))

    def across(ref, lead, sources, targets, send, recv, first):
        copies = []
        for d in range(2):
            src = ref.at[(slice(None),) * lead + (pl.ds(*sources[d]), slice(None))]
            dst = ref.at[(slice(None),) * lead + (pl.ds(*targets[d]), slice(None))]
            copies.append(
                pltpu.make_async_remote_copy(
                    src_ref=src, dst_ref=dst, send_sem=send.at[first + d], recv_sem=recv.at[first + d],
                    device_id=beside[d], device_id_type=MESH,
                )
            )
        for copy in copies:
            copy.start()
        return copies

    def fine(ref, lead, n, first):
        return across(
            ref, lead, ((O1 + 32 - n, n), (O1, n)), ((O1 - n, n), (O1 + 32, n)), a_send, a_recv, first
        )

    wide = ((O2, 16), (O2, 16)), ((O2 - 16, 16), (O2 + 16, 16))
    a_copies = fine(u1a, 2, 6, 0) + fine(f1, 2, 5, 2) + fine(s1, 1, 5, 4)
    a_late = fine(onehot, 0, 4, 6)
    b_early = across(s2, 1, *wide, b_send, b_recv, 0)
    for copy in a_copies:
        copy.wait_recv()

    step_size(t1, s1, O1 - 8, 6, 4, 1.0)
    section(u1b, u1a, u1a, f1, s1, t1, O1 - 8, 6, 4, 1.0, 1.0 / 3.0)
    section(u1c, u1a, u1b, f1, s1, t1, O1 - 4, 5, 4, 1.0, 0.5)
    section(u1b, u1a, u1c, f1, s1, t1, O1 - 4, 5, 4, 1.0, 1.0)

    target = jnp.where(row == 0, 127, 0)
    at_target = jnp.zeros((8, 128), jnp.int32) + target
    variable = (lane - 64 * row) // 8
    inside = lane >= 64 * row
    swap[...] = jnp.zeros((8, 128), jnp.float32)

    def residual(r):
        here = pl.ds(r, 8)
        _, out_l = apply_l(u1b, s1, r, 4, 1.0)
        mixed = jnp.zeros((8, 128), jnp.float32)
        for v in range(V):
            rest = [f1[v, t, here, :] - out_l[v][t] for t in range(4)]
            for t in range(4):
                u1c[v, t, here, :] = rest[t]
            face = jnp.take_along_axis(jnp.where(row == 0, rest[3], rest[0]), at_target, axis=1)
            mixed = jnp.where((variable == v) & inside, face, mixed)
        swap[...] += mixed * onehot[here, :]

    loop(O1, 4, residual)
    total = jnp.sum(swap[...], axis=0, keepdims=True)
    comb[0:1, :] = total
    to_core = pltpu.make_async_remote_copy(
        src_ref=comb.at[0:1, :], dst_ref=swapped.at[0:1, :], send_sem=g_send.at[0], recv_sem=g_recv.at[0],
        device_id=(1 - row, b), device_id_type=MESH,
    )
    to_core.start()

    for k, r in enumerate((-1, 7, 9)):
        for v in range(V):
            tiles = coarsen_rows(lambda t, rows, v=v: u1b[v, t, rows, :], O1 + 2 * r, 4, pick)
            for t in range(2):
                u2a[v, t, pl.ds(O2 + r, 8), :] = tiles[t]
    for r in (0, 8):
        for v in range(V):
            tiles = coarsen_rows(lambda t, rows, v=v: u1c[v, t, rows, :], O1 + 2 * r, 4, pick)
            for t in range(2):
                r2c[v, t, pl.ds(O2 + r, 8), :] = tiles[t]
    b_copies = across(
        u2a, 2, ((O2 - 1, 16), (O2 + 1, 16)), ((O2 - 17, 16), (O2 + 17, 16)), b_send, b_recv, 2
    )
    b_copies += across(r2c, 2, *wide, b_send, b_recv, 4)

    to_core.wait_recv()
    both = comb[0:1, :] + swapped[0:1, :]
    comb[1:2, :] = both
    zrows[pl.ds(z, 1), :] = both
    z_copies = [
        pltpu.make_async_remote_copy(
            src_ref=comb.at[1:2, :], dst_ref=zrows.at[pl.ds(z, 1), :], send_sem=g_send.at[1],
            recv_sem=g_recv.at[1], device_id=device, device_id_type=MESH,
        )
        for device in z_peers
    ]
    for copy in z_copies:
        copy.start()
    z_all = pltpu.make_async_remote_copy(
        src_ref=zrows.at[0 : NZ - 1, :], dst_ref=zrows.at[0 : NZ - 1, :], send_sem=g_send.at[1],
        recv_sem=g_recv.at[1], device_id=z_peers[0], device_id_type=MESH,
    )
    z_all.wait_recv()
    table[me] = zrows[...]
    t_copies = [
        pltpu.make_async_remote_copy(
            src_ref=zrows, dst_ref=table.at[me], send_sem=g_send.at[2],
            recv_sem=g_recv.at[2], device_id=device, device_id_type=MESH,
        )
        for device in xy_peers
    ]
    for copy in t_copies:
        copy.start()
    t_all = pltpu.make_async_remote_copy(
        src_ref=table.at[0 : NX * NY - 1], dst_ref=table.at[0 : NX * NY - 1], send_sem=g_send.at[2],
        recv_sem=g_recv.at[2], device_id=xy_peers[0], device_id_type=MESH,
    )

    for copy in b_early + b_copies:
        copy.wait_recv()
    step_size(t2, s2, O2 - 16, 6, 2, 0.25)
    portion = 1.0 / 3.0

    def middle_first(r):
        here = pl.ds(r, 8)
        centre, out_l = apply_l(u2a, s2, r, 2, 0.25)
        for t in range(2):
            tau = t2[t, here, :] * portion
            for v in range(V):
                rest = r2c[v, t, here, :]
                f2[v, t, here, :] = out_l[v][t] + rest
                u2b[v, t, here, :] = centre[v][t] + tau * rest

    loop(O2 - 16, 6, middle_first)
    section(u2c, u2a, u2b, f2, s2, t2, O2 - 16, 6, 2, 0.25, 0.5)
    section(u2b, u2a, u2c, f2, s2, t2, O2 - 16, 6, 2, 0.25, 1.0)

    def middle_rest(r):
        here = pl.ds(r, 8)
        _, out_l = apply_l(u2b, s2, r, 2, 0.25)
        for t in range(2):
            for v in range(V):
                u2c[v, t, here, :] = f2[v, t, here, :] - out_l[v][t]

    loop(O2 - 12, 5, middle_rest)

    for k in range(3):
        r, f = O3 - 8 + 8 * k, O2 - 16 + 16 * k
        here = pl.ds(r, 8)
        s3[0, here, :] = coarsen_rows(lambda t, rows: s2[t, rows, :], f, 2, pick)[0]
        t3[0, here, :] = 0.8 / (s3[0, here, :] + 1.75)
        for v in range(V):
            u3a[v, 0, here, :] = coarsen_rows(lambda t, rows, v=v: u2b[v, t, rows, :], f, 2, pick)[0]
            r3c[v, 0, here, :] = coarsen_rows(lambda t, rows, v=v: u2c[v, t, rows, :], f, 2, pick)[0]

    def coarse_first(r):
        here = pl.ds(r, 8)
        centre, out_l = apply_l(u3a, s3, r, 1, 0.0625)
        tau = t3[0, here, :] * 0.25
        for v in range(V):
            rest = r3c[v, 0, here, :]
            f3[v, 0, here, :] = out_l[v][0] + rest
            u3b[v, 0, here, :] = centre[v][0] + tau * rest

    loop(O3 - 8, 3, coarse_first)
    section(u3c, u3a, u3b, f3, s3, t3, O3 - 8, 3, 1, 0.0625, 1.0 / 3.0)
    section(u3b, u3a, u3c, f3, s3, t3, O3 - 4, 2, 1, 0.0625, 0.5)
    section(u3c, u3a, u3b, f3, s3, t3, O3 - 4, 2, 1, 0.0625, 1.0)

    spread = [lane // 2, 64 + lane // 2]
    for k in range(2):
        r, f = O3 - 4 + 8 * k, O2 - 8 + 16 * k
        for v in range(V):
            gain = u3c[v, 0, pl.ds(r, 8), :] - u3a[v, 0, pl.ds(r, 8), :]
            for t in range(2):
                more = jnp.take_along_axis(gain, spread[t], axis=1)
                for odd in range(2):
                    rows = pl.ds(f + odd, 8, stride=2)
                    u2d[v, t, rows, :] = u2b[v, t, rows, :] + more

    section(u2b, u2d, u2d, f2, s2, t2, O2 - 4, 3, 2, 0.25, 1.0 / 3.0)
    section(u2c, u2d, u2b, f2, s2, t2, O2 - 4, 3, 2, 0.25, 0.5)
    section(u2b, u2d, u2c, f2, s2, t2, O2 - 4, 3, 2, 0.25, 1.0)

    for r in (-2, 6, 10):
        f = O1 + 2 * r
        for v in range(V):
            for half in range(2):
                here = pl.ds(O2 + r, 8)
                gain = u2b[v, half, here, :] - u2a[v, half, here, :]
                for part in range(2):
                    t = 2 * half + part
                    more = jnp.take_along_axis(gain, spread[part], axis=1)
                    for odd in range(2):
                        rows = pl.ds(f + odd, 8, stride=2)
                        u1d[v, t, rows, :] = u1b[v, t, rows, :] + more

    for copy in a_late:
        copy.wait_recv()
    t_all.wait_recv()

    turn = jnp.where(row == 0, offset[0], 1024 - offset[0])
    index = rows_of()
    cell_own = 8 * b + index
    near_own = lax.rem(b + NB - 1 + index, NB)
    cell_other = (cell_own + turn) & 1023
    near_other = (near_own + turn) & 1023

    def chosen(block):
        block = block & 127
        place = ((block >> 5) * 4 + (block & 3)) * 8 + ((block >> 2) & 7)
        return (place == lane).astype(jnp.float32)

    wanted = jnp.concatenate(
        [chosen(cell_own), chosen(near_own), chosen(cell_other), chosen(near_other)], axis=0
    )
    found = jnp.dot(
        wanted, table[...].reshape(NB, 128), precision=HIGH, preferred_element_type=jnp.float32
    )
    turned = pltpu.roll(found, 64, 1)
    own = jnp.where(row == 0, found[0:16], turned[0:16])
    other = jnp.where(row == 0, turned[16:32], found[16:32])
    valid = lane < 40
    picked = jnp.where(valid & (low == (b // 16)), own[0:8], 0.0) + jnp.where(
        valid & (low == (cell_other >> 7)), other[0:8], 0.0
    )
    summed = (index == lane // 8).astype(jnp.float32)
    cells = lax.dot_general(
        summed, picked, (((1,), (1,)), ((), ())), precision=HIGH, preferred_element_type=jnp.float32
    )
    scale8 = jnp.zeros((8, 8), jnp.float32)
    for k in range(8):
        scale8 = jnp.where(lanes((8, 8)) == k, weight[0, 8 * b + k], scale8)
    cells = cells * scale8
    for v in range(V):
        loop_out[v] = cells[v : v + 1]

    rotate = (lane & ~7) | ((lane + (near_other >> 7)) & 7)
    corr = jnp.where(
        valid, wrow[...] * (own[8:16] + jnp.take_along_axis(other[8:16], rotate, axis=1)), 0.0
    )
    swap[...] = corr
    first_col = (lane == 0) & (row == 1)
    last_col = (lane == 127) & (row == 0)
    for k in range(5):
        r = O1 - 4 + 8 * k
        here = pl.ds(r, 8)
        near = index + r
        if k == 0:
            table_row = jnp.where(near < O1, swap[0:1, :], swap[1:2, :])
        elif k == 4:
            table_row = jnp.where(near < O1 + 32, swap[1:2, :], swap[2:3, :])
        else:
            table_row = swap[1:2, :]
        terms = onehot[here, :] * table_row
        for hop in (4, 2, 1):
            terms = terms + pltpu.roll(terms, 128 - hop, 1)
        for v in range(V):
            fix = jnp.take_along_axis(terms, jnp.full((8, 128), 8 * v, jnp.int32), axis=1)
            u1d[v, 0, here, :] += jnp.where(first_col, fix, 0.0)
            u1d[v, 3, here, :] += jnp.where(last_col, fix, 0.0)

    section(u1c, u1d, u1d, f1, s1, t1, O1 - 4, 5, 4, 1.0, 1.0 / 3.0)
    section(u1b, u1d, u1c, f1, s1, t1, O1 - 4, 5, 4, 1.0, 0.5)
    section(outb, u1d, u1b, f1, s1, t1, O1, 4, 4, 1.0, 1.0, shift=O1)

    stores = [
        pltpu.make_async_copy(outb.at[:, t], out.at[0, :, :, pl.ds(t * 128, 128)], out_sem.at[t])
        for t in range(4)
    ]
    for copy in stores:
        copy.start()
    for copy in a_copies + a_late + b_early + b_copies + [to_core]:
        copy.wait_send()
    z_all.wait_send()
    t_all.wait_send()
    for copy in stores:
        copy.wait()


def body(state, forcing, sigma, partner, loop_weight, offset):
    f32 = jnp.float32
    fine, middle, coarse = (V, 4, R1, 128), (V, 2, R2, 128), (V, 1, R3, 128)
    buffers = [fine] * 5 + [(4, R1, 128)] * 2 + [(V, 4, 32, 128)]
    buffers += [middle] * 6 + [(2, R2, 128)] * 2
    buffers += [coarse] * 5 + [(1, R3, 128)] * 2
    buffers += [(R1, 128), (8, 128), (8, 128), (8, 128), (8, 128), (NZ, 128), (NX * NY, NZ, 128)]
    hbm = pl.BlockSpec(memory_space=pltpu.HBM)
    vmem = pl.BlockSpec(memory_space=pltpu.VMEM)
    dma = pltpu.SemaphoreType.DMA
    placed = (state, forcing, sigma, partner.reshape(1, 1, 32), loop_weight)
    solved, corrected = pl.pallas_call(
        kernel,
        out_shape=(
            pltpu.VMEM((1, V, 32, 512), f32),
            pltpu.VMEM((V, 1, 8), f32),
        ),
        in_specs=[hbm] * 5 + [pl.BlockSpec(memory_space=pltpu.SMEM)],
        out_specs=(vmem, vmem),
        scratch_shapes=[pltpu.VMEM(shape, f32) for shape in buffers]
        + [pltpu.SMEM((1, 1, 32), jnp.int32), pltpu.SMEM((1, 1024), f32)]
        + [dma((15,)), dma((8,)), dma((8,)), dma((6,)), dma((6,)), dma((3,)), dma((3,)), dma((4,))],
        compiler_params=pltpu.CompilerParams(
            collective_id=0, has_side_effects=True, vmem_limit_bytes=40 * 1024 * 1024
        ),
        name="fas_cycle",
    )(*[pltpu.with_memory_space_constraint(x, pltpu.HBM) for x in placed], offset)
    return solved, corrected.reshape(1, V, 8)


def solution(mesh):
    placed = (
        P("row", None, "blk", None),
        P("row", None, "blk", None),
        P("row", "blk", None),
        P("row", "blk", None),
        P("row", None),
        P(),
    )
    return jax.shard_map(
        body,
        mesh=mesh,
        in_specs=placed,
        out_specs=(P("row", None, "blk", None), P("row", None, "blk")),
        check_vma=False,
    )
```

```python
import jax
import jax.numpy as jnp
from jax import lax
from jax.experimental import pallas as pl
from jax.experimental.pallas import tpu as pltpu
from jax.sharding import PartitionSpec as P

MESH = pl.DeviceIdType.MESH
V = 5
NB = 128
O1, R1 = 16, 64
O2, R2 = 24, 64
O3, R3 = 16, 40
NY, NZ, NX = 4, 8, 4
HIGH = lax.Precision.HIGHEST


def loop(first, tiles, body):
    if isinstance(first, tuple):
        low, second, third, high = first

        def strips(k, carry):
            body(low + k * (second - low))
            body(third + k * (high - third))
            return carry

        lax.fori_loop(0, 2, strips, 0)
        return

    def step(k, carry):
        body(first + 8 * k)
        return carry

    lax.fori_loop(0, tiles, step, 0, unroll=2 if tiles % 2 == 0 else 1)


def lanes(shape=(8, 128)):
    return lax.broadcasted_iota(jnp.int32, shape, 1)


def rows_of(shape=(8, 128)):
    return lax.broadcasted_iota(jnp.int32, shape, 0)


def apply_l(u_ref, s_ref, r, nt, scale):
    lane = lanes()
    first, last = lane == 0, lane == 127
    here = pl.ds(r, 8)
    centre = [[u_ref[v, t, here, :] for t in range(nt)] for v in range(V)]
    out = [[None] * nt for _ in range(V)]
    diag = []
    for t in range(nt):
        q = centre[0][t] * centre[0][t]
        for v in range(1, V):
            q = q + centre[v][t] * centre[v][t]
        q = q * (1.0 / V)
        diag.append((s_ref[t, here, :] + 4.0 * scale) + (0.5 * q) / (1.0 + q))
    for v in range(V):
        ahead = [pltpu.roll(centre[v][t], 127, 1) for t in range(nt)]
        behind = [pltpu.roll(centre[v][t], 1, 1) for t in range(nt)]
        for t in range(nt):
            right = jnp.where(last, ahead[t + 1] if t + 1 < nt else 0.0, ahead[t])
            left = jnp.where(first, behind[t - 1] if t > 0 else 0.0, behind[t])
            near = (right + left) + (
                u_ref[v, t, pl.ds(r - 1, 8), :] + u_ref[v, t, pl.ds(r + 1, 8), :]
            )
            if scale != 1.0:
                near = scale * near
            out[v][t] = diag[t] * centre[v][t] - near
    return centre, out


def section(dst, start, src, f_ref, s_ref, tau_ref, first, tiles, nt, scale, portion):
    def body(r):
        here = pl.ds(r, 8)
        _, out = apply_l(src, s_ref, r, nt, scale)
        for t in range(nt):
            tau = tau_ref[t, here, :] * portion
            for v in range(V):
                dst[v, t, here, :] = start[v, t, here, :] + tau * (
                    f_ref[v, t, here, :] - out[v][t]
                )

    loop(first, tiles, body)


def step_size(tau_ref, s_ref, first, tiles, nt, scale):
    def body(r):
        for t in range(nt):
            tau_ref[t, pl.ds(r, 8), :] = 0.8 / (s_ref[t, pl.ds(r, 8), :] + (4.0 * scale + 1.5))

    loop(first, tiles, body)


def halved(a, b, pick):
    lane = lanes()
    mixed = jnp.where(lane % 2 == 0, a + pltpu.roll(a, 127, 1), b + pltpu.roll(b, 1, 1))
    return jnp.take_along_axis(mixed, pick, axis=1)


def pair_pick():
    lane = lanes()
    return jnp.where(lane < 64, 2 * lane, 2 * lane - 127)


def coarsen_rows(get, f, nt, pick):
    pairs = [get(t, pl.ds(f, 8, stride=2)) + get(t, pl.ds(f + 1, 8, stride=2)) for t in range(nt)]
    if nt == 1:
        return [halved(pairs[0], jnp.zeros_like(pairs[0]), pick) * 0.25]
    return [halved(pairs[2 * t], pairs[2 * t + 1], pick) * 0.25 for t in range(nt // 2)]


def kernel(
    state, forcing, sigma, partner_in, weight_in, offset, out, loop_out,
    u1a, u1b, u1c, u1d, u1e, f1, s1, t1,
    u2a, u2b, u2c, u2d, r2c, f2, s2, t2,
    u3a, u3b, u3c, r3c, f3, s3, t3,
    onehot, wrow, swap, swapped, comb, zrows, table, partner, weight,
    load_sem, a_send, a_recv, b_send, b_recv, g_send, g_recv,
):
    row = lax.axis_index("row")
    b = lax.axis_index("blk")
    right, left = lax.rem(b + 1, NB), lax.rem(b + NB - 1, NB)
    y, z, x = b // 32, lax.rem(b // 4, NZ), lax.rem(b, NX)
    me = y * NX + x
    beside = [(row, right), (row, left)]
    z_peers = [(row, y * 32 + lax.rem(z + d, NZ) * 4 + x) for d in range(1, NZ)]
    xy_peers = [
        (row, lax.rem(y + dy, NY) * 32 + z * 4 + lax.rem(x + dx, NX))
        for dy in range(NY)
        for dx in range(NX)
        if dx or dy
    ]
    partners = beside + [(1 - row, b)] + z_peers + xy_peers
    barrier = pltpu.get_barrier_semaphore()
    for device in partners:
        pl.semaphore_signal(barrier, inc=1, device_id=device, device_id_type=MESH)

    loads = []
    for t in range(4):
        cols = pl.ds(t * 128, 128)
        own = pl.ds(O1, 32)
        loads.append((sigma.at[0, :, cols], s1.at[t, own, :]))
        loads.append((state.at[0, :, :, cols], u1a.at[:, t, own, :]))
        loads.append((forcing.at[0, :, :, cols], f1.at[:, t, own, :]))
    loads = [(partner_in, partner), (weight_in, weight)] + loads
    loads = [pltpu.make_async_copy(src, dst, load_sem.at[i]) for i, (src, dst) in enumerate(loads)]
    for copy in loads:
        copy.start()
    for copy in loads[:2]:
        copy.wait()

    lane = lanes()
    pick = pair_pick()
    low = lane % 8
    for k in range(4):
        slot = jnp.zeros((8, 128), jnp.int32)
        for i in range(8):
            slot = jnp.where(rows_of() == i, partner[0, 0, 8 * k + i] & 7, slot)
        onehot[pl.ds(O1 + 8 * k, 8), :] = (slot == low).astype(jnp.float32)
    weights = jnp.zeros((8, 128), jnp.float32)
    for d, block in enumerate((left, b, right)):
        for p in range(8):
            weights = jnp.where((rows_of() == d) & (low == p), weight[0, p * NB + block], weights)
    wrow[...] = weights

    for copy in loads[2:]:
        copy.wait()
    for k in range(2):
        r = O2 + 8 * k
        for t, tile in enumerate(coarsen_rows(lambda t, rows: s1[t, rows, :], O1 + 16 * k, 4, pick)):
            s2[t, pl.ds(r, 8), :] = tile
    pl.semaphore_wait(barrier, len(partners))

    def across(ref, lead, sources, targets, send, recv, first):
        copies = []
        for d in range(2):
            src = ref.at[(slice(None),) * lead + (pl.ds(*sources[d]), slice(None))]
            dst = ref.at[(slice(None),) * lead + (pl.ds(*targets[d]), slice(None))]
            copies.append(
                pltpu.make_async_remote_copy(
                    src_ref=src, dst_ref=dst, send_sem=send.at[first + d], recv_sem=recv.at[first + d],
                    device_id=beside[d], device_id_type=MESH,
                )
            )
        for copy in copies:
            copy.start()
        return copies

    def fine(ref, lead, n, first):
        return across(
            ref, lead, ((O1 + 32 - n, n), (O1, n)), ((O1 - n, n), (O1 + 32, n)), a_send, a_recv, first
        )

    wide = ((O2, 16), (O2, 16)), ((O2 - 16, 16), (O2 + 16, 16))
    a_copies = fine(u1a, 2, 6, 0) + fine(f1, 2, 5, 2) + fine(s1, 1, 5, 4)
    a_late = fine(onehot, 0, 4, 6)
    b_early = across(s2, 1, *wide, b_send, b_recv, 0)
    step_size(t1, s1, O1, 4, 4, 1.0)
    section(u1b, u1a, u1a, f1, s1, t1, O1 + 4, 3, 4, 1.0, 1.0 / 3.0)
    section(u1c, u1a, u1b, f1, s1, t1, O1 + 8, 2, 4, 1.0, 0.5)
    section(u1e, u1a, u1c, f1, s1, t1, O1 + 12, 1, 4, 1.0, 1.0)
    for copy in a_copies:
        copy.wait_recv()
    step_size(t1, s1, O1 - 8, 1, 4, 1.0)
    step_size(t1, s1, O1 + 32, 1, 4, 1.0)
    strips = dict(f_ref=f1, s_ref=s1, tau_ref=t1, nt=4, scale=1.0)
    section(u1b, u1a, u1a, first=(O1 - 8, O1 - 4, O1 + 28, O1 + 32), tiles=4, portion=1.0 / 3.0, **strips)
    section(u1c, u1a, u1b, first=(O1 - 4, O1, O1 + 24, O1 + 28), tiles=4, portion=0.5, **strips)
    section(u1e, u1a, u1c, first=(O1 - 4, O1 + 4, O1 + 20, O1 + 28), tiles=4, portion=1.0, **strips)

    target = jnp.where(row == 0, 127, 0)
    at_target = jnp.zeros((8, 128), jnp.int32) + target
    variable = (lane - 64 * row) // 8
    inside = lane >= 64 * row
    swap[...] = jnp.zeros((8, 128), jnp.float32)

    def residual(r):
        here = pl.ds(r, 8)
        _, out_l = apply_l(u1e, s1, r, 4, 1.0)
        mixed = jnp.zeros((8, 128), jnp.float32)
        for v in range(V):
            rest = [f1[v, t, here, :] - out_l[v][t] for t in range(4)]
            for t in range(4):
                u1c[v, t, here, :] = rest[t]
            face = jnp.take_along_axis(jnp.where(row == 0, rest[3], rest[0]), at_target, axis=1)
            mixed = jnp.where((variable == v) & inside, face, mixed)
        swap[...] += mixed * onehot[here, :]

    loop(O1, 4, residual)
    total = jnp.sum(swap[...], axis=0, keepdims=True)
    comb[0:1, :] = total
    to_core = pltpu.make_async_remote_copy(
        src_ref=comb.at[0:1, :], dst_ref=swapped.at[0:1, :], send_sem=g_send.at[0], recv_sem=g_recv.at[0],
        device_id=(1 - row, b), device_id_type=MESH,
    )
    to_core.start()

    for k, r in enumerate((-1, 7, 9)):
        for v in range(V):
            tiles = coarsen_rows(lambda t, rows, v=v: u1e[v, t, rows, :], O1 + 2 * r, 4, pick)
            for t in range(2):
                u2a[v, t, pl.ds(O2 + r, 8), :] = tiles[t]
    for r in (0, 8):
        for v in range(V):
            tiles = coarsen_rows(lambda t, rows, v=v: u1c[v, t, rows, :], O1 + 2 * r, 4, pick)
            for t in range(2):
                r2c[v, t, pl.ds(O2 + r, 8), :] = tiles[t]
    b_copies = across(
        u2a, 2, ((O2 - 1, 16), (O2 + 1, 16)), ((O2 - 17, 16), (O2 + 17, 16)), b_send, b_recv, 2
    )
    b_copies += across(r2c, 2, *wide, b_send, b_recv, 4)

    to_core.wait_recv()
    both = comb[0:1, :] + swapped[0:1, :]
    comb[1:2, :] = both
    zrows[pl.ds(z, 1), :] = both
    z_copies = [
        pltpu.make_async_remote_copy(
            src_ref=comb.at[1:2, :], dst_ref=zrows.at[pl.ds(z, 1), :], send_sem=g_send.at[1],
            recv_sem=g_recv.at[1], device_id=device, device_id_type=MESH,
        )
        for device in z_peers
    ]
    for copy in z_copies:
        copy.start()
    z_all = pltpu.make_async_remote_copy(
        src_ref=zrows.at[0 : NZ - 1, :], dst_ref=zrows.at[0 : NZ - 1, :], send_sem=g_send.at[1],
        recv_sem=g_recv.at[1], device_id=z_peers[0], device_id_type=MESH,
    )
    z_all.wait_recv()
    table[me] = zrows[...]
    t_copies = [
        pltpu.make_async_remote_copy(
            src_ref=zrows, dst_ref=table.at[me], send_sem=g_send.at[2],
            recv_sem=g_recv.at[2], device_id=device, device_id_type=MESH,
        )
        for device in xy_peers
    ]
    for copy in t_copies:
        copy.start()
    t_all = pltpu.make_async_remote_copy(
        src_ref=table.at[0 : NX * NY - 1], dst_ref=table.at[0 : NX * NY - 1], send_sem=g_send.at[2],
        recv_sem=g_recv.at[2], device_id=xy_peers[0], device_id_type=MESH,
    )

    for copy in b_early:
        copy.wait_recv()
    step_size(t2, s2, O2 - 16, 6, 2, 0.25)
    for k in range(3):
        here = pl.ds(O3 - 8 + 8 * k, 8)
        s3[0, here, :] = coarsen_rows(lambda t, rows: s2[t, rows, :], O2 - 16 + 16 * k, 2, pick)[0]
        t3[0, here, :] = 0.8 / (s3[0, here, :] + 1.75)
    for copy in b_copies:
        copy.wait_recv()
    portion = 1.0 / 3.0

    def middle_first(r):
        here = pl.ds(r, 8)
        centre, out_l = apply_l(u2a, s2, r, 2, 0.25)
        for t in range(2):
            tau = t2[t, here, :] * portion
            for v in range(V):
                rest = r2c[v, t, here, :]
                f2[v, t, here, :] = out_l[v][t] + rest
                u2b[v, t, here, :] = centre[v][t] + tau * rest

    loop(O2 - 16, 6, middle_first)
    section(u2c, u2a, u2b, f2, s2, t2, O2 - 16, 6, 2, 0.25, 0.5)
    section(u2b, u2a, u2c, f2, s2, t2, O2 - 16, 6, 2, 0.25, 1.0)

    def middle_rest(r):
        here = pl.ds(r, 8)
        _, out_l = apply_l(u2b, s2, r, 2, 0.25)
        for t in range(2):
            for v in range(V):
                u2c[v, t, here, :] = f2[v, t, here, :] - out_l[v][t]

    loop(O2 - 12, 5, middle_rest)

    for k in range(3):
        r, f = O3 - 8 + 8 * k, O2 - 16 + 16 * k
        here = pl.ds(r, 8)
        for v in range(V):
            u3a[v, 0, here, :] = coarsen_rows(lambda t, rows, v=v: u2b[v, t, rows, :], f, 2, pick)[0]
            r3c[v, 0, here, :] = coarsen_rows(lambda t, rows, v=v: u2c[v, t, rows, :], f, 2, pick)[0]

    def coarse_first(r):
        here = pl.ds(r, 8)
        centre, out_l = apply_l(u3a, s3, r, 1, 0.0625)
        tau = t3[0, here, :] * 0.25
        for v in range(V):
            rest = r3c[v, 0, here, :]
            f3[v, 0, here, :] = out_l[v][0] + rest
            u3b[v, 0, here, :] = centre[v][0] + tau * rest

    loop(O3 - 8, 3, coarse_first)
    section(u3c, u3a, u3b, f3, s3, t3, O3 - 8, 3, 1, 0.0625, 1.0 / 3.0)
    section(u3b, u3a, u3c, f3, s3, t3, O3 - 4, 2, 1, 0.0625, 0.5)
    section(u3c, u3a, u3b, f3, s3, t3, O3 - 4, 2, 1, 0.0625, 1.0)

    spread = [lane // 2, 64 + lane // 2]
    for k in range(2):
        r, f = O3 - 4 + 8 * k, O2 - 8 + 16 * k
        for v in range(V):
            gain = u3c[v, 0, pl.ds(r, 8), :] - u3a[v, 0, pl.ds(r, 8), :]
            for t in range(2):
                more = jnp.take_along_axis(gain, spread[t], axis=1)
                for odd in range(2):
                    rows = pl.ds(f + odd, 8, stride=2)
                    u2d[v, t, rows, :] = u2b[v, t, rows, :] + more

    section(u2b, u2d, u2d, f2, s2, t2, O2 - 4, 3, 2, 0.25, 1.0 / 3.0)
    section(u2c, u2d, u2b, f2, s2, t2, O2 - 4, 3, 2, 0.25, 0.5)
    section(u2b, u2d, u2c, f2, s2, t2, O2 - 4, 3, 2, 0.25, 1.0)

    for r in (-2, 6, 10):
        f = O1 + 2 * r
        for v in range(V):
            for half in range(2):
                here = pl.ds(O2 + r, 8)
                gain = u2b[v, half, here, :] - u2a[v, half, here, :]
                for part in range(2):
                    t = 2 * half + part
                    more = jnp.take_along_axis(gain, spread[part], axis=1)
                    for odd in range(2):
                        rows = pl.ds(f + odd, 8, stride=2)
                        u1d[v, t, rows, :] = u1e[v, t, rows, :] + more

    for copy in a_late:
        copy.wait_recv()
    t_all.wait_recv()

    turn = jnp.where(row == 0, offset[0], 1024 - offset[0])
    index = rows_of()
    cell_own = 8 * b + index
    near_own = lax.rem(b + NB - 1 + index, NB)
    cell_other = (cell_own + turn) & 1023
    near_other = (near_own + turn) & 1023

    def chosen(block):
        block = block & 127
        place = ((block >> 5) * 4 + (block & 3)) * 8 + ((block >> 2) & 7)
        return (place == lane).astype(jnp.float32)

    wanted = jnp.concatenate(
        [chosen(cell_own), chosen(near_own), chosen(cell_other), chosen(near_other)], axis=0
    )
    found = jnp.dot(
        wanted, table[...].reshape(NB, 128), precision=HIGH, preferred_element_type=jnp.float32
    )
    turned = pltpu.roll(found, 64, 1)
    own = jnp.where(row == 0, found[0:16], turned[0:16])
    other = jnp.where(row == 0, turned[16:32], found[16:32])
    valid = lane < 40
    picked = jnp.where(valid & (low == (b // 16)), own[0:8], 0.0) + jnp.where(
        valid & (low == (cell_other >> 7)), other[0:8], 0.0
    )
    summed = (index == lane // 8).astype(jnp.float32)
    cells = lax.dot_general(
        summed, picked, (((1,), (1,)), ((), ())), precision=HIGH, preferred_element_type=jnp.float32
    )
    scale8 = jnp.zeros((8, 8), jnp.float32)
    for k in range(8):
        scale8 = jnp.where(lanes((8, 8)) == k, weight[0, 8 * b + k], scale8)
    cells = cells * scale8
    for v in range(V):
        loop_out[v] = cells[v : v + 1]

    rotate = (lane & ~7) | ((lane + (near_other >> 7)) & 7)
    corr = jnp.where(
        valid, wrow[...] * (own[8:16] + jnp.take_along_axis(other[8:16], rotate, axis=1)), 0.0
    )
    swap[...] = corr
    first_col = (lane == 0) & (row == 1)
    last_col = (lane == 127) & (row == 0)
    for k in range(5):
        r = O1 - 4 + 8 * k
        here = pl.ds(r, 8)
        near = index + r
        if k == 0:
            table_row = jnp.where(near < O1, swap[0:1, :], swap[1:2, :])
        elif k == 4:
            table_row = jnp.where(near < O1 + 32, swap[1:2, :], swap[2:3, :])
        else:
            table_row = swap[1:2, :]
        terms = onehot[here, :] * table_row
        for hop in (4, 2, 1):
            terms = terms + pltpu.roll(terms, 128 - hop, 1)
        for v in range(V):
            fix = jnp.take_along_axis(terms, jnp.full((8, 128), 8 * v, jnp.int32), axis=1)
            u1d[v, 0, here, :] += jnp.where(first_col, fix, 0.0)
            u1d[v, 3, here, :] += jnp.where(last_col, fix, 0.0)

    section(u1c, u1d, u1d, f1, s1, t1, O1 - 4, 5, 4, 1.0, 1.0 / 3.0)
    section(u1b, u1d, u1c, f1, s1, t1, O1 - 4, 5, 4, 1.0, 0.5)

    def last(r):
        here = pl.ds(r, 8)
        _, out_l = apply_l(u1b, s1, r, 4, 1.0)
        for t in range(4):
            tau = t1[t, here, :]
            for v in range(V):
                out[0, v, pl.ds(r - O1, 8), 128 * t : 128 * t + 128] = u1d[v, t, here, :] + tau * (
                    f1[v, t, here, :] - out_l[v][t]
                )

    loop(O1, 4, last)
    for copy in a_copies + a_late + b_early + b_copies + [to_core]:
        copy.wait_send()
    z_all.wait_send()
    t_all.wait_send()


def write_out(solved, corrected, out, loop_out, sem):
    copies = [
        pltpu.make_async_copy(solved, out, sem.at[0]),
        pltpu.make_async_copy(corrected, loop_out, sem.at[1]),
    ]
    for copy in copies:
        copy.start()
    for copy in copies:
        copy.wait()


def body(state, forcing, sigma, partner, loop_weight, offset):
    f32 = jnp.float32
    fine, middle, coarse = (V, 4, R1, 128), (V, 2, R2, 128), (V, 1, R3, 128)
    buffers = [fine] * 6 + [(4, R1, 128)] * 2
    buffers += [middle] * 6 + [(2, R2, 128)] * 2
    buffers += [coarse] * 5 + [(1, R3, 128)] * 2
    buffers += [(R1, 128), (8, 128), (8, 128), (8, 128), (8, 128), (NZ, 128), (NX * NY, NZ, 128)]
    hbm = pl.BlockSpec(memory_space=pltpu.HBM)
    vmem = pl.BlockSpec(memory_space=pltpu.VMEM)
    dma = pltpu.SemaphoreType.DMA
    placed = (state, forcing, sigma, partner.reshape(1, 1, 32), loop_weight)
    solved, corrected = pl.pallas_call(
        kernel,
        out_shape=(
            pltpu.VMEM((1, V, 32, 512), f32),
            pltpu.VMEM((V, 1, 8), f32),
        ),
        in_specs=[hbm] * 5 + [pl.BlockSpec(memory_space=pltpu.SMEM)],
        out_specs=(vmem, vmem),
        scratch_shapes=[pltpu.VMEM(shape, f32) for shape in buffers]
        + [pltpu.SMEM((1, 1, 32), jnp.int32), pltpu.SMEM((1, 1024), f32)]
        + [dma((15,)), dma((8,)), dma((8,)), dma((6,)), dma((6,)), dma((3,)), dma((3,))],
        compiler_params=pltpu.CompilerParams(
            collective_id=0, has_side_effects=True, vmem_limit_bytes=40 * 1024 * 1024
        ),
        name="fas_cycle",
    )(*[pltpu.with_memory_space_constraint(x, pltpu.HBM) for x in placed], offset)
    solved = pltpu.with_memory_space_constraint(solved, pltpu.VMEM)
    corrected = pltpu.with_memory_space_constraint(corrected, pltpu.VMEM)
    solved, corrected = pl.pallas_call(
        write_out,
        out_shape=(
            jax.ShapeDtypeStruct((1, V, 32, 512), f32),
            jax.ShapeDtypeStruct((V, 1, 8), f32),
        ),
        in_specs=[vmem] * 2,
        out_specs=(pl.BlockSpec(memory_space=pl.ANY),) * 2,
        scratch_shapes=[dma((2,))],
        compiler_params=pltpu.CompilerParams(vmem_limit_bytes=40 * 1024 * 1024),
        name="write_out",
    )(solved, corrected)
    return solved, corrected.reshape(1, V, 8)


def solution(mesh):
    placed = (
        P("row", None, "blk", None),
        P("row", None, "blk", None),
        P("row", "blk", None),
        P("row", "blk", None),
        P("row", None),
        P(),
    )
    return jax.shard_map(
        body,
        mesh=mesh,
        in_specs=placed,
        out_specs=(P("row", None, "blk", None), P("row", None, "blk")),
        check_vma=False,
    )
```

```python
import jax
import jax.numpy as jnp
from jax import lax
from jax.experimental import pallas as pl
from jax.experimental.pallas import tpu as pltpu
from jax.sharding import PartitionSpec as P

MESH = pl.DeviceIdType.MESH
V = 5
NB = 128
O1, R1 = 16, 64
O2, R2 = 24, 64
O3, R3 = 16, 40
NY, NZ, NX = 4, 8, 4
HIGH = lax.Precision.HIGHEST


def loop(first, tiles, body):
    if isinstance(first, tuple):
        low, second, third, high = first

        def strips(k, carry):
            body(low + k * (second - low))
            body(third + k * (high - third))
            return carry

        lax.fori_loop(0, 2, strips, 0)
        return

    def step(k, carry):
        body(first + 8 * k)
        return carry

    lax.fori_loop(0, tiles, step, 0, unroll=2 if tiles == 4 else 3 if tiles == 6 else tiles)


def lanes(shape=(8, 128)):
    return lax.broadcasted_iota(jnp.int32, shape, 1)


def rows_of(shape=(8, 128)):
    return lax.broadcasted_iota(jnp.int32, shape, 0)


def apply_l(u_ref, s_ref, r, nt, scale):
    lane = lanes()
    first, last = lane == 0, lane == 127
    here = pl.ds(r, 8)
    centre = [[u_ref[v, t, here, :] for t in range(nt)] for v in range(V)]
    out = [[None] * nt for _ in range(V)]
    diag = []
    for t in range(nt):
        q = centre[0][t] * centre[0][t]
        for v in range(1, V):
            q = q + centre[v][t] * centre[v][t]
        q = q * (1.0 / V)
        diag.append((s_ref[t, here, :] + 4.0 * scale) + (0.5 * q) / (1.0 + q))
    for v in range(V):
        ahead = [pltpu.roll(centre[v][t], 127, 1) for t in range(nt)]
        behind = [pltpu.roll(centre[v][t], 1, 1) for t in range(nt)]
        for t in range(nt):
            right = jnp.where(last, ahead[t + 1] if t + 1 < nt else 0.0, ahead[t])
            left = jnp.where(first, behind[t - 1] if t > 0 else 0.0, behind[t])
            near = (right + left) + (
                u_ref[v, t, pl.ds(r - 1, 8), :] + u_ref[v, t, pl.ds(r + 1, 8), :]
            )
            if scale != 1.0:
                near = scale * near
            out[v][t] = diag[t] * centre[v][t] - near
    return centre, out


def section(dst, start, src, f_ref, s_ref, tau_ref, first, tiles, nt, scale, portion):
    def body(r):
        here = pl.ds(r, 8)
        _, out = apply_l(src, s_ref, r, nt, scale)
        for t in range(nt):
            tau = tau_ref[t, here, :] * portion
            for v in range(V):
                dst[v, t, here, :] = start[v, t, here, :] + tau * (
                    f_ref[v, t, here, :] - out[v][t]
                )

    loop(first, tiles, body)


def step_size(tau_ref, s_ref, first, tiles, nt, scale):
    def body(r):
        for t in range(nt):
            tau_ref[t, pl.ds(r, 8), :] = 0.8 / (s_ref[t, pl.ds(r, 8), :] + (4.0 * scale + 1.5))

    loop(first, tiles, body)


def halved(a, b, pick):
    lane = lanes()
    mixed = jnp.where(lane % 2 == 0, a + pltpu.roll(a, 127, 1), b + pltpu.roll(b, 1, 1))
    return jnp.take_along_axis(mixed, pick, axis=1)


def pair_pick():
    lane = lanes()
    return jnp.where(lane < 64, 2 * lane, 2 * lane - 127)


def coarsen_rows(get, f, nt, pick):
    pairs = [get(t, pl.ds(f, 8, stride=2)) + get(t, pl.ds(f + 1, 8, stride=2)) for t in range(nt)]
    if nt == 1:
        return [halved(pairs[0], jnp.zeros_like(pairs[0]), pick) * 0.25]
    return [halved(pairs[2 * t], pairs[2 * t + 1], pick) * 0.25 for t in range(nt // 2)]


def kernel(
    state, forcing, sigma, partner_in, weight_in, offset, out, loop_out,
    u1a, u1b, u1c, u1d, u1e, f1, s1, t1,
    u2a, u2b, u2c, u2d, r2c, f2, s2, t2,
    u3a, u3b, u3c, r3c, f3, s3, t3,
    onehot, wrow, swap, swapped, comb, zrows, table, partner, weight,
    load_sem, a_send, a_recv, b_send, b_recv, g_send, g_recv,
):
    row = lax.axis_index("row")
    b = lax.axis_index("blk")
    right, left = lax.rem(b + 1, NB), lax.rem(b + NB - 1, NB)
    y, z, x = b // 32, lax.rem(b // 4, NZ), lax.rem(b, NX)
    me = y * NX + x
    beside = [(row, right), (row, left)]
    z_peers = [(row, y * 32 + lax.rem(z + d, NZ) * 4 + x) for d in range(1, NZ)]
    xy_peers = [
        (row, lax.rem(y + dy, NY) * 32 + z * 4 + lax.rem(x + dx, NX))
        for dy in range(NY)
        for dx in range(NX)
        if dx or dy
    ]
    partners = beside + [(1 - row, b)] + z_peers + xy_peers
    barrier = pltpu.get_barrier_semaphore()
    for device in partners:
        pl.semaphore_signal(barrier, inc=1, device_id=device, device_id_type=MESH)

    loads = []
    for t in range(4):
        cols = pl.ds(t * 128, 128)
        own = pl.ds(O1, 32)
        loads.append((sigma.at[0, :, cols], s1.at[t, own, :]))
        loads.append((state.at[0, :, :, cols], u1a.at[:, t, own, :]))
        loads.append((forcing.at[0, :, :, cols], f1.at[:, t, own, :]))
    loads = [(partner_in, partner), (weight_in, weight)] + loads
    loads = [pltpu.make_async_copy(src, dst, load_sem.at[i]) for i, (src, dst) in enumerate(loads)]
    for copy in loads:
        copy.start()
    for copy in loads[:2]:
        copy.wait()

    lane = lanes()
    pick = pair_pick()
    low = lane % 8
    for k in range(4):
        slot = jnp.zeros((8, 128), jnp.int32)
        for i in range(8):
            slot = jnp.where(rows_of() == i, partner[0, 0, 8 * k + i] & 7, slot)
        onehot[pl.ds(O1 + 8 * k, 8), :] = (slot == low).astype(jnp.float32)
    weights = jnp.zeros((8, 128), jnp.float32)
    for d, block in enumerate((left, b, right)):
        for p in range(8):
            weights = jnp.where((rows_of() == d) & (low == p), weight[0, p * NB + block], weights)
    wrow[...] = weights

    for copy in loads[2:]:
        copy.wait()
    for k in range(2):
        r = O2 + 8 * k
        for t, tile in enumerate(coarsen_rows(lambda t, rows: s1[t, rows, :], O1 + 16 * k, 4, pick)):
            s2[t, pl.ds(r, 8), :] = tile
    pl.semaphore_wait(barrier, len(partners))

    def across(ref, lead, sources, targets, send, recv, first):
        copies = []
        for d in range(2):
            src = ref.at[(slice(None),) * lead + (pl.ds(*sources[d]), slice(None))]
            dst = ref.at[(slice(None),) * lead + (pl.ds(*targets[d]), slice(None))]
            copies.append(
                pltpu.make_async_remote_copy(
                    src_ref=src, dst_ref=dst, send_sem=send.at[first + d], recv_sem=recv.at[first + d],
                    device_id=beside[d], device_id_type=MESH,
                )
            )
        for copy in copies:
            copy.start()
        return copies

    def fine(ref, lead, n, first):
        return across(
            ref, lead, ((O1 + 32 - n, n), (O1, n)), ((O1 - n, n), (O1 + 32, n)), a_send, a_recv, first
        )

    wide = ((O2, 16), (O2, 16)), ((O2 - 16, 16), (O2 + 16, 16))
    a_copies = fine(u1a, 2, 6, 0) + fine(f1, 2, 5, 2) + fine(s1, 1, 5, 4)
    a_late = fine(onehot, 0, 4, 6)
    b_early = across(s2, 1, *wide, b_send, b_recv, 0)
    step_size(t1, s1, O1, 4, 4, 1.0)
    section(u1b, u1a, u1a, f1, s1, t1, O1 + 4, 3, 4, 1.0, 1.0 / 3.0)
    section(u1c, u1a, u1b, f1, s1, t1, O1 + 8, 2, 4, 1.0, 0.5)
    section(u1e, u1a, u1c, f1, s1, t1, O1 + 12, 1, 4, 1.0, 1.0)
    for copy in a_copies:
        copy.wait_recv()
    step_size(t1, s1, O1 - 8, 1, 4, 1.0)
    step_size(t1, s1, O1 + 32, 1, 4, 1.0)
    strips = dict(f_ref=f1, s_ref=s1, tau_ref=t1, nt=4, scale=1.0)
    section(u1b, u1a, u1a, first=(O1 - 8, O1 - 4, O1 + 28, O1 + 32), tiles=4, portion=1.0 / 3.0, **strips)
    section(u1c, u1a, u1b, first=(O1 - 4, O1, O1 + 24, O1 + 28), tiles=4, portion=0.5, **strips)
    section(u1e, u1a, u1c, first=(O1 - 4, O1 + 4, O1 + 20, O1 + 28), tiles=4, portion=1.0, **strips)

    for k, r in enumerate((-1, 7, 9)):
        for v in range(V):
            tiles = coarsen_rows(lambda t, rows, v=v: u1e[v, t, rows, :], O1 + 2 * r, 4, pick)
            for t in range(2):
                u2a[v, t, pl.ds(O2 + r, 8), :] = tiles[t]
    b_copies = across(
        u2a, 2, ((O2 - 1, 16), (O2 + 1, 16)), ((O2 - 17, 16), (O2 + 17, 16)), b_send, b_recv, 2
    )
    target = jnp.where(row == 0, 127, 0)
    at_target = jnp.zeros((8, 128), jnp.int32) + target
    variable = (lane - 64 * row) // 8
    inside = lane >= 64 * row
    swap[...] = jnp.zeros((8, 128), jnp.float32)

    def residual(r):
        here = pl.ds(r, 8)
        _, out_l = apply_l(u1e, s1, r, 4, 1.0)
        mixed = jnp.zeros((8, 128), jnp.float32)
        for v in range(V):
            rest = [f1[v, t, here, :] - out_l[v][t] for t in range(4)]
            for t in range(4):
                u1c[v, t, here, :] = rest[t]
            face = jnp.take_along_axis(jnp.where(row == 0, rest[3], rest[0]), at_target, axis=1)
            mixed = jnp.where((variable == v) & inside, face, mixed)
        swap[...] += mixed * onehot[here, :]

    loop(O1, 4, residual)
    total = jnp.sum(swap[...], axis=0, keepdims=True)
    comb[0:1, :] = total
    to_core = pltpu.make_async_remote_copy(
        src_ref=comb.at[0:1, :], dst_ref=swapped.at[0:1, :], send_sem=g_send.at[0], recv_sem=g_recv.at[0],
        device_id=(1 - row, b), device_id_type=MESH,
    )
    to_core.start()

    for r in (0, 8):
        for v in range(V):
            tiles = coarsen_rows(lambda t, rows, v=v: u1c[v, t, rows, :], O1 + 2 * r, 4, pick)
            for t in range(2):
                r2c[v, t, pl.ds(O2 + r, 8), :] = tiles[t]
    b_copies += across(r2c, 2, *wide, b_send, b_recv, 4)

    to_core.wait_recv()
    both = comb[0:1, :] + swapped[0:1, :]
    comb[1:2, :] = both
    zrows[pl.ds(z, 1), :] = both
    z_copies = [
        pltpu.make_async_remote_copy(
            src_ref=comb.at[1:2, :], dst_ref=zrows.at[pl.ds(z, 1), :], send_sem=g_send.at[1],
            recv_sem=g_recv.at[1], device_id=device, device_id_type=MESH,
        )
        for device in z_peers
    ]
    for copy in z_copies:
        copy.start()
    z_all = pltpu.make_async_remote_copy(
        src_ref=zrows.at[0 : NZ - 1, :], dst_ref=zrows.at[0 : NZ - 1, :], send_sem=g_send.at[1],
        recv_sem=g_recv.at[1], device_id=z_peers[0], device_id_type=MESH,
    )
    z_all.wait_recv()
    table[me] = zrows[...]
    t_copies = [
        pltpu.make_async_remote_copy(
            src_ref=zrows, dst_ref=table.at[me], send_sem=g_send.at[2],
            recv_sem=g_recv.at[2], device_id=device, device_id_type=MESH,
        )
        for device in xy_peers
    ]
    for copy in t_copies:
        copy.start()
    t_all = pltpu.make_async_remote_copy(
        src_ref=table.at[0 : NX * NY - 1], dst_ref=table.at[0 : NX * NY - 1], send_sem=g_send.at[2],
        recv_sem=g_recv.at[2], device_id=xy_peers[0], device_id_type=MESH,
    )

    for copy in b_early:
        copy.wait_recv()
    step_size(t2, s2, O2 - 16, 6, 2, 0.25)
    for k in range(3):
        here = pl.ds(O3 - 8 + 8 * k, 8)
        s3[0, here, :] = coarsen_rows(lambda t, rows: s2[t, rows, :], O2 - 16 + 16 * k, 2, pick)[0]
        t3[0, here, :] = 0.8 / (s3[0, here, :] + 1.75)
    for copy in b_copies:
        copy.wait_recv()
    portion = 1.0 / 3.0

    def middle_first(r):
        here = pl.ds(r, 8)
        centre, out_l = apply_l(u2a, s2, r, 2, 0.25)
        for t in range(2):
            tau = t2[t, here, :] * portion
            for v in range(V):
                rest = r2c[v, t, here, :]
                f2[v, t, here, :] = out_l[v][t] + rest
                u2b[v, t, here, :] = centre[v][t] + tau * rest

    loop(O2 - 16, 6, middle_first)
    section(u2c, u2a, u2b, f2, s2, t2, O2 - 16, 6, 2, 0.25, 0.5)
    section(u2b, u2a, u2c, f2, s2, t2, O2 - 16, 6, 2, 0.25, 1.0)

    def middle_rest(r):
        here = pl.ds(r, 8)
        _, out_l = apply_l(u2b, s2, r, 2, 0.25)
        for t in range(2):
            for v in range(V):
                u2c[v, t, here, :] = f2[v, t, here, :] - out_l[v][t]

    loop(O2 - 12, 5, middle_rest)

    for k in range(3):
        r, f = O3 - 8 + 8 * k, O2 - 16 + 16 * k
        here = pl.ds(r, 8)
        for v in range(V):
            u3a[v, 0, here, :] = coarsen_rows(lambda t, rows, v=v: u2b[v, t, rows, :], f, 2, pick)[0]
            r3c[v, 0, here, :] = coarsen_rows(lambda t, rows, v=v: u2c[v, t, rows, :], f, 2, pick)[0]

    def coarse_first(r):
        here = pl.ds(r, 8)
        centre, out_l = apply_l(u3a, s3, r, 1, 0.0625)
        tau = t3[0, here, :] * 0.25
        for v in range(V):
            rest = r3c[v, 0, here, :]
            f3[v, 0, here, :] = out_l[v][0] + rest
            u3b[v, 0, here, :] = centre[v][0] + tau * rest

    loop(O3 - 8, 3, coarse_first)
    section(u3c, u3a, u3b, f3, s3, t3, O3 - 8, 3, 1, 0.0625, 1.0 / 3.0)
    section(u3b, u3a, u3c, f3, s3, t3, O3 - 4, 2, 1, 0.0625, 0.5)
    section(u3c, u3a, u3b, f3, s3, t3, O3 - 4, 2, 1, 0.0625, 1.0)

    spread = [lane // 2, 64 + lane // 2]
    for k in range(2):
        r, f = O3 - 4 + 8 * k, O2 - 8 + 16 * k
        for v in range(V):
            gain = u3c[v, 0, pl.ds(r, 8), :] - u3a[v, 0, pl.ds(r, 8), :]
            for t in range(2):
                more = jnp.take_along_axis(gain, spread[t], axis=1)
                for odd in range(2):
                    rows = pl.ds(f + odd, 8, stride=2)
                    u2d[v, t, rows, :] = u2b[v, t, rows, :] + more

    section(u2b, u2d, u2d, f2, s2, t2, O2 - 4, 3, 2, 0.25, 1.0 / 3.0)
    section(u2c, u2d, u2b, f2, s2, t2, O2 - 4, 3, 2, 0.25, 0.5)
    section(u2b, u2d, u2c, f2, s2, t2, O2 - 4, 3, 2, 0.25, 1.0)

    for r in (-2, 6, 10):
        f = O1 + 2 * r
        for v in range(V):
            for half in range(2):
                here = pl.ds(O2 + r, 8)
                gain = u2b[v, half, here, :] - u2a[v, half, here, :]
                for part in range(2):
                    t = 2 * half + part
                    more = jnp.take_along_axis(gain, spread[part], axis=1)
                    for odd in range(2):
                        rows = pl.ds(f + odd, 8, stride=2)
                        u1d[v, t, rows, :] = u1e[v, t, rows, :] + more

    for copy in a_late:
        copy.wait_recv()
    t_all.wait_recv()

    turn = jnp.where(row == 0, offset[0], 1024 - offset[0])
    index = rows_of()
    cell_own = 8 * b + index
    near_own = lax.rem(b + NB - 1 + index, NB)
    cell_other = (cell_own + turn) & 1023
    near_other = (near_own + turn) & 1023

    def chosen(block):
        block = block & 127
        place = ((block >> 5) * 4 + (block & 3)) * 8 + ((block >> 2) & 7)
        return (place == lane).astype(jnp.float32)

    wanted = jnp.concatenate(
        [chosen(cell_own), chosen(near_own), chosen(cell_other), chosen(near_other)], axis=0
    )
    found = jnp.dot(
        wanted, table[...].reshape(NB, 128), precision=HIGH, preferred_element_type=jnp.float32
    )
    turned = pltpu.roll(found, 64, 1)
    own = jnp.where(row == 0, found[0:16], turned[0:16])
    other = jnp.where(row == 0, turned[16:32], found[16:32])
    valid = lane < 40
    picked = jnp.where(valid & (low == (b // 16)), own[0:8], 0.0) + jnp.where(
        valid & (low == (cell_other >> 7)), other[0:8], 0.0
    )
    summed = (index == lane // 8).astype(jnp.float32)
    cells = lax.dot_general(
        summed, picked, (((1,), (1,)), ((), ())), precision=HIGH, preferred_element_type=jnp.float32
    )
    scale8 = jnp.zeros((8, 8), jnp.float32)
    for k in range(8):
        scale8 = jnp.where(lanes((8, 8)) == k, weight[0, 8 * b + k], scale8)
    cells = cells * scale8
    for v in range(V):
        loop_out[v] = cells[v : v + 1]

    rotate = (lane & ~7) | ((lane + (near_other >> 7)) & 7)
    corr = jnp.where(
        valid, wrow[...] * (own[8:16] + jnp.take_along_axis(other[8:16], rotate, axis=1)), 0.0
    )
    swap[...] = corr
    first_col = (lane == 0) & (row == 1)
    last_col = (lane == 127) & (row == 0)
    for k in range(5):
        r = O1 - 4 + 8 * k
        here = pl.ds(r, 8)
        near = index + r
        if k == 0:
            table_row = jnp.where(near < O1, swap[0:1, :], swap[1:2, :])
        elif k == 4:
            table_row = jnp.where(near < O1 + 32, swap[1:2, :], swap[2:3, :])
        else:
            table_row = swap[1:2, :]
        terms = onehot[here, :] * table_row
        for hop in (4, 2, 1):
            terms = terms + pltpu.roll(terms, 128 - hop, 1)
        for v in range(V):
            fix = jnp.take_along_axis(terms, jnp.full((8, 128), 8 * v, jnp.int32), axis=1)
            u1d[v, 0, here, :] += jnp.where(first_col, fix, 0.0)
            u1d[v, 3, here, :] += jnp.where(last_col, fix, 0.0)

    section(u1c, u1d, u1d, f1, s1, t1, O1 - 4, 5, 4, 1.0, 1.0 / 3.0)
    section(u1b, u1d, u1c, f1, s1, t1, O1 - 4, 5, 4, 1.0, 0.5)

    def last(r):
        here = pl.ds(r, 8)
        _, out_l = apply_l(u1b, s1, r, 4, 1.0)
        for t in range(4):
            tau = t1[t, here, :]
            for v in range(V):
                out[0, v, pl.ds(r - O1, 8), 128 * t : 128 * t + 128] = u1d[v, t, here, :] + tau * (
                    f1[v, t, here, :] - out_l[v][t]
                )

    loop(O1, 4, last)
    for copy in a_copies + a_late + b_early + b_copies + [to_core]:
        copy.wait_send()
    z_all.wait_send()
    t_all.wait_send()


def write_out(solved, corrected, out, loop_out, sem):
    copies = [
        pltpu.make_async_copy(solved, out, sem.at[0]),
        pltpu.make_async_copy(corrected, loop_out, sem.at[1]),
    ]
    for copy in copies:
        copy.start()
    for copy in copies:
        copy.wait()


def body(state, forcing, sigma, partner, loop_weight, offset):
    f32 = jnp.float32
    fine, middle, coarse = (V, 4, R1, 128), (V, 2, R2, 128), (V, 1, R3, 128)
    buffers = [fine] * 6 + [(4, R1, 128)] * 2
    buffers += [middle] * 6 + [(2, R2, 128)] * 2
    buffers += [coarse] * 5 + [(1, R3, 128)] * 2
    buffers += [(R1, 128), (8, 128), (8, 128), (8, 128), (8, 128), (NZ, 128), (NX * NY, NZ, 128)]
    hbm = pl.BlockSpec(memory_space=pltpu.HBM)
    vmem = pl.BlockSpec(memory_space=pltpu.VMEM)
    dma = pltpu.SemaphoreType.DMA
    placed = (state, forcing, sigma, partner.reshape(1, 1, 32), loop_weight)
    solved, corrected = pl.pallas_call(
        kernel,
        out_shape=(
            pltpu.VMEM((1, V, 32, 512), f32),
            pltpu.VMEM((V, 1, 8), f32),
        ),
        in_specs=[hbm] * 5 + [pl.BlockSpec(memory_space=pltpu.SMEM)],
        out_specs=(vmem, vmem),
        scratch_shapes=[pltpu.VMEM(shape, f32) for shape in buffers]
        + [pltpu.SMEM((1, 1, 32), jnp.int32), pltpu.SMEM((1, 1024), f32)]
        + [dma((15,)), dma((8,)), dma((8,)), dma((6,)), dma((6,)), dma((3,)), dma((3,))],
        compiler_params=pltpu.CompilerParams(
            collective_id=0, has_side_effects=True, vmem_limit_bytes=40 * 1024 * 1024
        ),
        name="fas_cycle",
    )(*[pltpu.with_memory_space_constraint(x, pltpu.HBM) for x in placed], offset)
    solved = pltpu.with_memory_space_constraint(solved, pltpu.VMEM)
    corrected = pltpu.with_memory_space_constraint(corrected, pltpu.VMEM)
    solved, corrected = pl.pallas_call(
        write_out,
        out_shape=(
            jax.ShapeDtypeStruct((1, V, 32, 512), f32),
            jax.ShapeDtypeStruct((V, 1, 8), f32),
        ),
        in_specs=[vmem] * 2,
        out_specs=(pl.BlockSpec(memory_space=pl.ANY),) * 2,
        scratch_shapes=[dma((2,))],
        compiler_params=pltpu.CompilerParams(vmem_limit_bytes=40 * 1024 * 1024),
        name="write_out",
    )(solved, corrected)
    return solved, corrected.reshape(1, V, 8)


def solution(mesh):
    placed = (
        P("row", None, "blk", None),
        P("row", None, "blk", None),
        P("row", "blk", None),
        P("row", "blk", None),
        P("row", None),
        P(),
    )
    return jax.shard_map(
        body,
        mesh=mesh,
        in_specs=placed,
        out_specs=(P("row", None, "blk", None), P("row", None, "blk")),
        check_vma=False,
    )
```

```python
import jax
import jax.numpy as jnp
from jax import lax
from jax.experimental import pallas as pl
from jax.experimental.pallas import tpu as pltpu
from jax.sharding import PartitionSpec as P

MESH = pl.DeviceIdType.MESH
V = 5
NB = 128
O1, R1 = 16, 64
O2, R2 = 24, 64
O3, R3 = 16, 40
NY, NZ, NX = 4, 8, 4
HIGH = lax.Precision.HIGHEST


def loop(first, tiles, body):
    if isinstance(first, tuple):
        low, second, third, high = first

        def strips(k, carry):
            body(low + k * (second - low))
            body(third + k * (high - third))
            return carry

        lax.fori_loop(0, 2, strips, 0)
        return

    def step(k, carry):
        body(first + 8 * k)
        return carry

    lax.fori_loop(0, tiles, step, 0, unroll=2 if tiles == 4 else 3 if tiles == 6 else tiles)


def lanes(shape=(8, 128)):
    return lax.broadcasted_iota(jnp.int32, shape, 1)


def rows_of(shape=(8, 128)):
    return lax.broadcasted_iota(jnp.int32, shape, 0)


def apply_l(u_ref, s_ref, r, nt, scale):
    lane = lanes()
    first, last = lane == 0, lane == 127
    here = pl.ds(r, 8)
    centre = [[u_ref[v, t, here, :] for t in range(nt)] for v in range(V)]
    out = [[None] * nt for _ in range(V)]
    diag = []
    for t in range(nt):
        q = centre[0][t] * centre[0][t]
        for v in range(1, V):
            q = q + centre[v][t] * centre[v][t]
        q = q * (1.0 / V)
        diag.append((s_ref[t, here, :] + 4.0 * scale) + (0.5 * q) / (1.0 + q))
    for v in range(V):
        ahead = [pltpu.roll(centre[v][t], 127, 1) for t in range(nt)]
        behind = [pltpu.roll(centre[v][t], 1, 1) for t in range(nt)]
        for t in range(nt):
            right = jnp.where(last, ahead[t + 1] if t + 1 < nt else 0.0, ahead[t])
            left = jnp.where(first, behind[t - 1] if t > 0 else 0.0, behind[t])
            near = (right + left) + (
                u_ref[v, t, pl.ds(r - 1, 8), :] + u_ref[v, t, pl.ds(r + 1, 8), :]
            )
            if scale != 1.0:
                near = scale * near
            out[v][t] = diag[t] * centre[v][t] - near
    return centre, out


def section(dst, start, src, f_ref, s_ref, tau_ref, first, tiles, nt, scale, portion):
    def body(r):
        here = pl.ds(r, 8)
        _, out = apply_l(src, s_ref, r, nt, scale)
        for t in range(nt):
            tau = tau_ref[t, here, :] * portion
            for v in range(V):
                dst[v, t, here, :] = start[v, t, here, :] + tau * (
                    f_ref[v, t, here, :] - out[v][t]
                )

    loop(first, tiles, body)


def step_size(tau_ref, s_ref, first, tiles, nt, scale):
    def body(r):
        for t in range(nt):
            tau_ref[t, pl.ds(r, 8), :] = 0.8 / (s_ref[t, pl.ds(r, 8), :] + (4.0 * scale + 1.5))

    loop(first, tiles, body)


def halved(a, b, pick):
    lane = lanes()
    mixed = jnp.where(lane % 2 == 0, a + pltpu.roll(a, 127, 1), b + pltpu.roll(b, 1, 1))
    return jnp.take_along_axis(mixed, pick, axis=1)


def pair_pick():
    lane = lanes()
    return jnp.where(lane < 64, 2 * lane, 2 * lane - 127)


def coarsen_rows(get, f, nt, pick):
    pairs = [get(t, pl.ds(f, 8, stride=2)) + get(t, pl.ds(f + 1, 8, stride=2)) for t in range(nt)]
    if nt == 1:
        return [halved(pairs[0], jnp.zeros_like(pairs[0]), pick) * 0.25]
    return [halved(pairs[2 * t], pairs[2 * t + 1], pick) * 0.25 for t in range(nt // 2)]


def kernel(
    state, forcing, sigma, partner_in, weight_in, offset, out, loop_out,
    u1a, u1b, u1c, u1d, u1e, f1, s1, t1,
    u2a, u2b, u2c, u2d, r2c, f2, s2, t2,
    u3a, u3b, u3c, r3c, f3, s3, t3,
    onehot, wrow, swap, swapped, comb, zrows, table, partner, weight,
    load_sem, a_send, a_recv, b_send, b_recv, g_send, g_recv,
):
    row = lax.axis_index("row")
    b = lax.axis_index("blk")
    right, left = lax.rem(b + 1, NB), lax.rem(b + NB - 1, NB)
    y, z, x = b // 32, lax.rem(b // 4, NZ), lax.rem(b, NX)
    me = y * NX + x
    beside = [(row, right), (row, left)]
    z_peers = [(row, y * 32 + lax.rem(z + d, NZ) * 4 + x) for d in range(1, NZ)]
    xy_peers = [
        (row, lax.rem(y + dy, NY) * 32 + z * 4 + lax.rem(x + dx, NX))
        for dy in range(NY)
        for dx in range(NX)
        if dx or dy
    ]
    partners = beside + [(1 - row, b)] + z_peers + xy_peers
    barrier = pltpu.get_barrier_semaphore()
    for device in partners:
        pl.semaphore_signal(barrier, inc=1, device_id=device, device_id_type=MESH)

    loads = []
    for t in range(4):
        cols = pl.ds(t * 128, 128)
        own = pl.ds(O1, 32)
        loads.append((sigma.at[0, :, cols], s1.at[t, own, :]))
        loads.append((state.at[0, :, :, cols], u1a.at[:, t, own, :]))
        loads.append((forcing.at[0, :, :, cols], f1.at[:, t, own, :]))
    loads = [(partner_in, partner), (weight_in, weight)] + loads
    loads = [pltpu.make_async_copy(src, dst, load_sem.at[i]) for i, (src, dst) in enumerate(loads)]
    for copy in loads:
        copy.start()
    for copy in loads[:2]:
        copy.wait()

    lane = lanes()
    pick = pair_pick()
    low = lane % 8
    for k in range(4):
        slot = jnp.zeros((8, 128), jnp.int32)
        for i in range(8):
            slot = jnp.where(rows_of() == i, partner[0, 0, 8 * k + i] & 7, slot)
        onehot[pl.ds(O1 + 8 * k, 8), :] = (slot == low).astype(jnp.float32)
    weights = jnp.zeros((8, 128), jnp.float32)
    for d, block in enumerate((left, b, right)):
        for p in range(8):
            weights = jnp.where((rows_of() == d) & (low == p), weight[0, p * NB + block], weights)
    wrow[...] = weights

    for copy in loads[2:]:
        copy.wait()
    for k in range(2):
        r = O2 + 8 * k
        for t, tile in enumerate(coarsen_rows(lambda t, rows: s1[t, rows, :], O1 + 16 * k, 4, pick)):
            s2[t, pl.ds(r, 8), :] = tile
    pl.semaphore_wait(barrier, len(partners))

    def across(ref, lead, sources, targets, send, recv, first):
        copies = []
        for d in range(2):
            src = ref.at[(slice(None),) * lead + (pl.ds(*sources[d]), slice(None))]
            dst = ref.at[(slice(None),) * lead + (pl.ds(*targets[d]), slice(None))]
            copies.append(
                pltpu.make_async_remote_copy(
                    src_ref=src, dst_ref=dst, send_sem=send.at[first + d], recv_sem=recv.at[first + d],
                    device_id=beside[d], device_id_type=MESH,
                )
            )
        for copy in copies:
            copy.start()
        return copies

    def fine(ref, lead, n, first):
        return across(
            ref, lead, ((O1 + 32 - n, n), (O1, n)), ((O1 - n, n), (O1 + 32, n)), a_send, a_recv, first
        )

    wide = ((O2, 16), (O2, 16)), ((O2 - 16, 16), (O2 + 16, 16))
    a_copies = fine(u1a, 2, 6, 0) + fine(f1, 2, 5, 2) + fine(s1, 1, 5, 4)
    a_late = fine(onehot, 0, 4, 6)
    b_early = across(s2, 1, *wide, b_send, b_recv, 0)
    step_size(t1, s1, O1, 4, 4, 1.0)
    section(u1b, u1a, u1a, f1, s1, t1, O1 + 4, 3, 4, 1.0, 1.0 / 3.0)
    section(u1c, u1a, u1b, f1, s1, t1, O1 + 8, 2, 4, 1.0, 0.5)
    section(u1e, u1a, u1c, f1, s1, t1, O1 + 12, 1, 4, 1.0, 1.0)
    for copy in a_copies:
        copy.wait_recv()
    step_size(t1, s1, O1 - 8, 1, 4, 1.0)
    step_size(t1, s1, O1 + 32, 1, 4, 1.0)
    strips = dict(f_ref=f1, s_ref=s1, tau_ref=t1, nt=4, scale=1.0)
    section(u1b, u1a, u1a, first=(O1 - 8, O1 - 4, O1 + 28, O1 + 32), tiles=4, portion=1.0 / 3.0, **strips)
    section(u1c, u1a, u1b, first=(O1 - 4, O1, O1 + 24, O1 + 28), tiles=4, portion=0.5, **strips)
    section(u1e, u1a, u1c, first=(O1 - 4, O1 + 4, O1 + 20, O1 + 28), tiles=4, portion=1.0, **strips)

    for k, r in enumerate((-1, 7, 9)):
        for v in range(V):
            tiles = coarsen_rows(lambda t, rows, v=v: u1e[v, t, rows, :], O1 + 2 * r, 4, pick)
            for t in range(2):
                u2a[v, t, pl.ds(O2 + r, 8), :] = tiles[t]
    b_copies = across(
        u2a, 2, ((O2 - 1, 16), (O2 + 1, 16)), ((O2 - 17, 16), (O2 + 17, 16)), b_send, b_recv, 2
    )
    target = jnp.where(row == 0, 127, 0)
    at_target = jnp.zeros((8, 128), jnp.int32) + target
    variable = (lane - 64 * row) // 8
    inside = lane >= 64 * row
    swap[...] = jnp.zeros((8, 128), jnp.float32)

    def residual(r):
        here = pl.ds(r, 8)
        _, out_l = apply_l(u1e, s1, r, 4, 1.0)
        mixed = jnp.zeros((8, 128), jnp.float32)
        for v in range(V):
            rest = [f1[v, t, here, :] - out_l[v][t] for t in range(4)]
            for t in range(4):
                u1c[v, t, here, :] = rest[t]
            face = jnp.take_along_axis(jnp.where(row == 0, rest[3], rest[0]), at_target, axis=1)
            mixed = jnp.where((variable == v) & inside, face, mixed)
        swap[...] += mixed * onehot[here, :]

    loop(O1, 4, residual)
    total = jnp.sum(swap[...], axis=0, keepdims=True)
    comb[0:1, :] = total
    to_core = pltpu.make_async_remote_copy(
        src_ref=comb.at[0:1, :], dst_ref=swapped.at[0:1, :], send_sem=g_send.at[0], recv_sem=g_recv.at[0],
        device_id=(1 - row, b), device_id_type=MESH,
    )
    to_core.start()

    for r in (0, 8):
        for v in range(V):
            tiles = coarsen_rows(lambda t, rows, v=v: u1c[v, t, rows, :], O1 + 2 * r, 4, pick)
            for t in range(2):
                r2c[v, t, pl.ds(O2 + r, 8), :] = tiles[t]
    b_copies += across(r2c, 2, *wide, b_send, b_recv, 4)

    to_core.wait_recv()
    both = comb[0:1, :] + swapped[0:1, :]
    comb[1:2, :] = both
    zrows[pl.ds(z, 1), :] = both
    z_copies = [
        pltpu.make_async_remote_copy(
            src_ref=comb.at[1:2, :], dst_ref=zrows.at[pl.ds(z, 1), :], send_sem=g_send.at[1],
            recv_sem=g_recv.at[1], device_id=device, device_id_type=MESH,
        )
        for device in z_peers
    ]
    for copy in z_copies:
        copy.start()
    z_all = pltpu.make_async_remote_copy(
        src_ref=zrows.at[0 : NZ - 1, :], dst_ref=zrows.at[0 : NZ - 1, :], send_sem=g_send.at[1],
        recv_sem=g_recv.at[1], device_id=z_peers[0], device_id_type=MESH,
    )
    z_all.wait_recv()
    table[me] = zrows[...]
    t_copies = [
        pltpu.make_async_remote_copy(
            src_ref=zrows, dst_ref=table.at[me], send_sem=g_send.at[2],
            recv_sem=g_recv.at[2], device_id=device, device_id_type=MESH,
        )
        for device in xy_peers
    ]
    for copy in t_copies:
        copy.start()
    t_all = pltpu.make_async_remote_copy(
        src_ref=table.at[0 : NX * NY - 1], dst_ref=table.at[0 : NX * NY - 1], send_sem=g_send.at[2],
        recv_sem=g_recv.at[2], device_id=xy_peers[0], device_id_type=MESH,
    )

    turn = jnp.where(row == 0, offset[0], 1024 - offset[0])
    index = rows_of()
    cell_own = 8 * b + index
    near_own = lax.rem(b + NB - 1 + index, NB)
    cell_other = (cell_own + turn) & 1023
    near_other = (near_own + turn) & 1023

    def chosen(block):
        block = block & 127
        place = ((block >> 5) * 4 + (block & 3)) * 8 + ((block >> 2) & 7)
        return (place == lane).astype(jnp.float32)

    wanted = jnp.concatenate(
        [chosen(cell_own), chosen(near_own), chosen(cell_other), chosen(near_other)], axis=0
    )
    scale8 = jnp.zeros((8, 8), jnp.float32)
    for k in range(8):
        scale8 = jnp.where(lanes((8, 8)) == k, weight[0, 8 * b + k], scale8)
    rotate = (lane & ~7) | ((lane + (near_other >> 7)) & 7)
    summed = (index == lane // 8).astype(jnp.float32)
    for copy in b_early:
        copy.wait_recv()
    step_size(t2, s2, O2 - 16, 6, 2, 0.25)
    for k in range(3):
        here = pl.ds(O3 - 8 + 8 * k, 8)
        s3[0, here, :] = coarsen_rows(lambda t, rows: s2[t, rows, :], O2 - 16 + 16 * k, 2, pick)[0]
        t3[0, here, :] = 0.8 / (s3[0, here, :] + 1.75)
    for copy in b_copies[0:2]:
        copy.wait_recv()

    def middle_l(r):
        here = pl.ds(r, 8)
        _, out_l = apply_l(u2a, s2, r, 2, 0.25)
        for t in range(2):
            for v in range(V):
                f2[v, t, here, :] = out_l[v][t]

    loop(O2 - 16, 6, middle_l)
    for copy in b_copies[2:4]:
        copy.wait_recv()
    portion = 1.0 / 3.0

    def middle_first(r):
        here = pl.ds(r, 8)
        for t in range(2):
            tau = t2[t, here, :] * portion
            for v in range(V):
                rest = r2c[v, t, here, :]
                f2[v, t, here, :] += rest
                u2b[v, t, here, :] = u2a[v, t, here, :] + tau * rest

    loop(O2 - 16, 6, middle_first)
    section(u2c, u2a, u2b, f2, s2, t2, O2 - 16, 6, 2, 0.25, 0.5)
    section(u2b, u2a, u2c, f2, s2, t2, O2 - 16, 6, 2, 0.25, 1.0)

    def middle_rest(r):
        here = pl.ds(r, 8)
        _, out_l = apply_l(u2b, s2, r, 2, 0.25)
        for t in range(2):
            for v in range(V):
                u2c[v, t, here, :] = f2[v, t, here, :] - out_l[v][t]

    loop(O2 - 12, 5, middle_rest)

    for k in range(3):
        r, f = O3 - 8 + 8 * k, O2 - 16 + 16 * k
        here = pl.ds(r, 8)
        for v in range(V):
            u3a[v, 0, here, :] = coarsen_rows(lambda t, rows, v=v: u2b[v, t, rows, :], f, 2, pick)[0]
            r3c[v, 0, here, :] = coarsen_rows(lambda t, rows, v=v: u2c[v, t, rows, :], f, 2, pick)[0]

    def coarse_first(r):
        here = pl.ds(r, 8)
        centre, out_l = apply_l(u3a, s3, r, 1, 0.0625)
        tau = t3[0, here, :] * 0.25
        for v in range(V):
            rest = r3c[v, 0, here, :]
            f3[v, 0, here, :] = out_l[v][0] + rest
            u3b[v, 0, here, :] = centre[v][0] + tau * rest

    loop(O3 - 8, 3, coarse_first)
    section(u3c, u3a, u3b, f3, s3, t3, O3 - 8, 3, 1, 0.0625, 1.0 / 3.0)
    section(u3b, u3a, u3c, f3, s3, t3, O3 - 4, 2, 1, 0.0625, 0.5)
    section(u3c, u3a, u3b, f3, s3, t3, O3 - 4, 2, 1, 0.0625, 1.0)

    spread = [lane // 2, 64 + lane // 2]
    for k in range(2):
        r, f = O3 - 4 + 8 * k, O2 - 8 + 16 * k
        for v in range(V):
            gain = u3c[v, 0, pl.ds(r, 8), :] - u3a[v, 0, pl.ds(r, 8), :]
            for t in range(2):
                more = jnp.take_along_axis(gain, spread[t], axis=1)
                for odd in range(2):
                    rows = pl.ds(f + odd, 8, stride=2)
                    u2d[v, t, rows, :] = u2b[v, t, rows, :] + more

    section(u2b, u2d, u2d, f2, s2, t2, O2 - 4, 3, 2, 0.25, 1.0 / 3.0)
    section(u2c, u2d, u2b, f2, s2, t2, O2 - 4, 3, 2, 0.25, 0.5)
    section(u2b, u2d, u2c, f2, s2, t2, O2 - 4, 3, 2, 0.25, 1.0)

    for r in (-2, 6, 10):
        f = O1 + 2 * r
        for v in range(V):
            for half in range(2):
                here = pl.ds(O2 + r, 8)
                gain = u2b[v, half, here, :] - u2a[v, half, here, :]
                for part in range(2):
                    t = 2 * half + part
                    more = jnp.take_along_axis(gain, spread[part], axis=1)
                    for odd in range(2):
                        rows = pl.ds(f + odd, 8, stride=2)
                        u1d[v, t, rows, :] = u1e[v, t, rows, :] + more

    for copy in a_late:
        copy.wait_recv()
    t_all.wait_recv()

    found = jnp.dot(
        wanted, table[...].reshape(NB, 128), precision=HIGH, preferred_element_type=jnp.float32
    )
    turned = pltpu.roll(found, 64, 1)
    own = jnp.where(row == 0, found[0:16], turned[0:16])
    other = jnp.where(row == 0, turned[16:32], found[16:32])
    valid = lane < 40
    picked = jnp.where(valid & (low == (b // 16)), own[0:8], 0.0) + jnp.where(
        valid & (low == (cell_other >> 7)), other[0:8], 0.0
    )
    cells = lax.dot_general(
        summed, picked, (((1,), (1,)), ((), ())), precision=HIGH, preferred_element_type=jnp.float32
    )
    cells = cells * scale8
    for v in range(V):
        loop_out[v] = cells[v : v + 1]

    corr = jnp.where(
        valid, wrow[...] * (own[8:16] + jnp.take_along_axis(other[8:16], rotate, axis=1)), 0.0
    )
    swap[...] = corr
    first_col = (lane == 0) & (row == 1)
    last_col = (lane == 127) & (row == 0)
    for k in range(5):
        r = O1 - 4 + 8 * k
        here = pl.ds(r, 8)
        near = index + r
        if k == 0:
            table_row = jnp.where(near < O1, swap[0:1, :], swap[1:2, :])
        elif k == 4:
            table_row = jnp.where(near < O1 + 32, swap[1:2, :], swap[2:3, :])
        else:
            table_row = swap[1:2, :]
        terms = onehot[here, :] * table_row
        for hop in (4, 2, 1):
            terms = terms + pltpu.roll(terms, 128 - hop, 1)
        for v in range(V):
            fix = jnp.take_along_axis(terms, jnp.full((8, 128), 8 * v, jnp.int32), axis=1)
            u1d[v, 0, here, :] += jnp.where(first_col, fix, 0.0)
            u1d[v, 3, here, :] += jnp.where(last_col, fix, 0.0)

    section(u1c, u1d, u1d, f1, s1, t1, O1 - 4, 5, 4, 1.0, 1.0 / 3.0)
    section(u1b, u1d, u1c, f1, s1, t1, O1 - 4, 5, 4, 1.0, 0.5)

    def last(r):
        here = pl.ds(r, 8)
        _, out_l = apply_l(u1b, s1, r, 4, 1.0)
        for t in range(4):
            tau = t1[t, here, :]
            for v in range(V):
                out[0, v, pl.ds(r - O1, 8), 128 * t : 128 * t + 128] = u1d[v, t, here, :] + tau * (
                    f1[v, t, here, :] - out_l[v][t]
                )

    loop(O1, 4, last)
    for copy in a_copies + a_late + b_early + b_copies + [to_core]:
        copy.wait_send()
    z_all.wait_send()
    t_all.wait_send()


def write_out(solved, corrected, out, loop_out, sem):
    copies = [
        pltpu.make_async_copy(solved, out, sem.at[0]),
        pltpu.make_async_copy(corrected, loop_out, sem.at[1]),
    ]
    for copy in copies:
        copy.start()
    for copy in copies:
        copy.wait()


def body(state, forcing, sigma, partner, loop_weight, offset):
    f32 = jnp.float32
    fine, middle, coarse = (V, 4, R1, 128), (V, 2, R2, 128), (V, 1, R3, 128)
    buffers = [fine] * 6 + [(4, R1, 128)] * 2
    buffers += [middle] * 6 + [(2, R2, 128)] * 2
    buffers += [coarse] * 5 + [(1, R3, 128)] * 2
    buffers += [(R1, 128), (8, 128), (8, 128), (8, 128), (8, 128), (NZ, 128), (NX * NY, NZ, 128)]
    hbm = pl.BlockSpec(memory_space=pltpu.HBM)
    vmem = pl.BlockSpec(memory_space=pltpu.VMEM)
    dma = pltpu.SemaphoreType.DMA
    placed = (state, forcing, sigma, partner.reshape(1, 1, 32), loop_weight)
    solved, corrected = pl.pallas_call(
        kernel,
        out_shape=(
            pltpu.VMEM((1, V, 32, 512), f32),
            pltpu.VMEM((V, 1, 8), f32),
        ),
        in_specs=[hbm] * 5 + [pl.BlockSpec(memory_space=pltpu.SMEM)],
        out_specs=(vmem, vmem),
        scratch_shapes=[pltpu.VMEM(shape, f32) for shape in buffers]
        + [pltpu.SMEM((1, 1, 32), jnp.int32), pltpu.SMEM((1, 1024), f32)]
        + [dma((15,)), dma((8,)), dma((8,)), dma((6,)), dma((6,)), dma((3,)), dma((3,))],
        compiler_params=pltpu.CompilerParams(
            collective_id=0, has_side_effects=True, vmem_limit_bytes=40 * 1024 * 1024
        ),
        name="fas_cycle",
    )(*[pltpu.with_memory_space_constraint(x, pltpu.HBM) for x in placed], offset)
    solved = pltpu.with_memory_space_constraint(solved, pltpu.VMEM)
    corrected = pltpu.with_memory_space_constraint(corrected, pltpu.VMEM)
    solved, corrected = pl.pallas_call(
        write_out,
        out_shape=(
            jax.ShapeDtypeStruct((1, V, 32, 512), f32),
            jax.ShapeDtypeStruct((V, 1, 8), f32),
        ),
        in_specs=[vmem] * 2,
        out_specs=(pl.BlockSpec(memory_space=pl.ANY),) * 2,
        scratch_shapes=[dma((2,))],
        compiler_params=pltpu.CompilerParams(vmem_limit_bytes=40 * 1024 * 1024),
        name="write_out",
    )(solved, corrected)
    return solved, corrected.reshape(1, V, 8)


def solution(mesh):
    placed = (
        P("row", None, "blk", None),
        P("row", None, "blk", None),
        P("row", "blk", None),
        P("row", "blk", None),
        P("row", None),
        P(),
    )
    return jax.shard_map(
        body,
        mesh=mesh,
        in_specs=placed,
        out_specs=(P("row", None, "blk", None), P("row", None, "blk")),
        check_vma=False,
    )
```
